128 devices in a mesh: grp: 4 (over x), fsdp: 32 (over y, z, core).
Axes of the slice: x: 4, y: 4, z: 4, core: 2. Of those that a mesh axis runs over, the one named last changes fastest.
Arguments:
- tokens: bfloat16 [8192, 4096], P('fsdp'), may hold values from -550 to 550
- attn_gain: float32 [4096], replicated, may hold values from 0.1 to 1.9
- ffn_gain: float32 [4096], replicated, may hold values from 0.1 to 1.9
- w_query: bfloat16 [4096, 4096], P('fsdp', 'grp'), may hold values from -2.421875 to 2.421875
- w_key: bfloat16 [4096, 256], P('fsdp'), may hold values from -0.078125 to 0.078125
- value_weight: bfloat16 [4096, 256], P('fsdp'), may hold values from -0.09375 to 0.09375
- w_out: bfloat16 [4096, 4096], P('grp', 'fsdp'), may hold values from -0.5 to 0.5
- routes: int32 [8192, 8], P('fsdp'), may hold values from 0 to 127, all different within a row; in each aligned block of 256 rows (0 to 255, 256 to 511, ...) at most 24 rows name the same one
- route_probs: bfloat16 [8192, 8], P('fsdp'), may hold values from 0.049804688 to 0.3984375
- w_gate_up: bfloat16 [128, 4096, 1536], P(('grp', 'fsdp')), may hold values from -0.09375 to 0.09375
- w_down: bfloat16 [128, 768, 4096], P(('grp', 'fsdp')), may hold values from -0.21875 to 0.21875
Outputs:
- attn_branch: bfloat16 [8192, 4096], P('fsdp')
- layer_out: bfloat16 [8192, 4096], P('fsdp', 'grp')
The draws below stay inside these ranges and needn't reach their ends.
Inputs may be any that keep to these rules, and one draw needn't show every extreme that they name: `routes`: each row names 8 different experts. Among the 256 rows of one device (aligned blocks), no expert is named more than 24 times, a bound that some block reaches.
All inputs are finite; a program needn't handle non-finite values.
Results may differ from the reference program's by a relative error of at most 0.015.
Values may be sent and summed in bfloat16 or wider, within the bound.
No kernel may reach another device: no remote copies, remote signals or barrier semaphores. Data moves between devices by JAX's collectives and lax.ppermute only.
A program may use at most 128 MiB of HBM per device.

```python
import math
import jax
import jax.numpy as jnp
import numpy as np
from jax import lax

MODEL_DIMENSION = 4096
QUERY_HEADS = 32
KEY_VALUE_HEADS = 2
HEAD_DIMENSION = 128
FFW = 768
TOPK = 8
TOK_DEV = 256
SEQUENCE_TOKENS = 8192
EXPERTS = 128
CAP = 24
N_GRP = 4
N_FSDP = 32


def common_keys(key):
    random_portion = jax.random.normal(jax.random.fold_in(key, 11), (MODEL_DIMENSION, KEY_VALUE_HEADS * HEAD_DIMENSION), jnp.float32)
    return jnp.clip(random_portion, -5.0, 5.0) / math.sqrt(MODEL_DIMENSION)


def draw_w_key(key, part):
    return common_keys(key).astype(jnp.bfloat16)


def draw_w_query(key, part):
    base_draw = jax.random.normal(jax.random.fold_in(key, 12), (MODEL_DIMENSION, QUERY_HEADS * HEAD_DIMENSION), jnp.float32)
    base_draw = jnp.clip(base_draw, -5.0, 5.0) / math.sqrt(MODEL_DIMENSION)
    return base_draw.astype(jnp.bfloat16)


def draw_tokens(key, part):
    base_draw = jnp.clip(jax.random.normal(jax.random.fold_in(key, 21), (SEQUENCE_TOKENS, MODEL_DIMENSION), jnp.float32), -5.0, 5.0)
    return base_draw.astype(jnp.bfloat16)


def levels(rng, shape, cuts, smallest, top_value):
    def one(dim, shards_of):
        draws = jax.random.uniform(jax.random.fold_in(jax.random.fold_in(rng, 6), dim), (shards_of,), jnp.float32, smallest / len(cuts), top_value / len(cuts))
        return jnp.repeat(jnp.exp(draws), shape[dim] // shards_of).reshape((-1,) + (1,) * (len(shape) - dim - 1))

    factor_of = one(*cuts[0])
    for cut in cuts[1:]:
        factor_of = factor_of * one(*cut)
    return factor_of


def shared_out(rng, own, number, rows, amount, top, most, slope):
    order = jax.random.permutation(rng, amount)
    heavy_load, common = shares(amount, rows * top, most, slope, True), shares(amount, rows * top, most, slope, False)
    places = jnp.arange(amount)

    def named(lengths, offset_by):
        used = int((lengths > 0).sum())
        fixed = max(1, used // 4)
        shifted = fixed + (places - fixed + offset_by * (used - fixed)) % max(1, amount - fixed)
        return jnp.zeros((amount,), jnp.int32).at[order[jnp.where(places < fixed, places, shifted)]].set(jnp.asarray(lengths, jnp.int32))

    lengths = jnp.where(number % 4 == 0, named(heavy_load, number // 4), named(common, number - number // 4 - 1))
    mixed = jax.random.permutation(jax.random.fold_in(own, 3), amount)
    giver, sink = mixed[0:amount // 2 * 2:2], mixed[1:amount // 2 * 2:2]
    margin = jnp.minimum(lengths[giver] - 1, most - lengths[sink]) // 2
    margin = jnp.where((giver == order[0]) | (sink == order[0]) | (lengths[sink] == 0), 0, jnp.maximum(margin, 0))
    shifted = jax.random.randint(jax.random.fold_in(own, 4), (amount // 2,), 0, 1 << 20) % (margin + 1)
    lengths = lengths.at[giver].add(-shifted).at[sink].add(shifted)
    labels = jnp.searchsorted(jnp.cumsum(lengths), jnp.arange(rows * top), side="right").astype(jnp.int32)
    listing = labels.reshape(top, rows).T
    listing = listing[jax.random.permutation(jax.random.fold_in(own, 1), rows)]
    offset_by = jax.random.randint(jax.random.fold_in(own, 2), (rows, 1), 0, top)
    return jnp.take_along_axis(listing, (jnp.arange(top)[None, :] + offset_by) % top, axis=1)


def shares(amount, total, limit, slope, full):
    weights = [(1 << 20) // math.isqrt(grade ** slope) + 1 for grade in range(1, amount + 1)]
    largest = limit if full else min(limit, max(-(-total // amount), total * weights[0] // sum(weights)))
    least = 1 if total - largest >= amount - 1 else 0
    holding, spare = [largest] + [least] * (amount - 1), total - largest - least * (amount - 1)
    while spare > 0:
        candidates = [i for i in range(1, amount) if holding[i] < largest] or [i for i in range(1, amount) if holding[i] < limit]
        whole, left = sum([weights[i] for i in candidates]), spare
        for i in candidates:
            extra = min(limit - holding[i], max(1, left * weights[i] // whole), spare)
            holding[i] = holding[i] + extra
            spare = spare - extra
    return np.array(holding)


def centred(own_key, extent, deviation, bound, shards=(), kind=jnp.bfloat16):
    drawn = jax.random.normal(own_key, extent, jnp.float32) * deviation
    if len(shards) > 0:
        drawn = levels(own_key, extent, shards, -0.22, 0.18) * drawn
    return jnp.clip(drawn, min=-bound, max=bound).astype(kind)


def setup_inputs(seed: int = 0) -> dict:
    streams_of = jax.random.split(jax.random.key(seed), 12)
    tokens = draw_tokens(jax.random.fold_in(streams_of[11], 71), 0)
    attn_gain = jnp.clip(1.0 + 0.18 * jax.random.normal(streams_of[1], (MODEL_DIMENSION,), jnp.float32), 0.1, 1.9)
    ffn_gain = jnp.clip(1.0 + 0.18 * jax.random.normal(streams_of[2], (MODEL_DIMENSION,), jnp.float32), 0.1, 1.9)
    w_query = draw_w_query(jax.random.fold_in(streams_of[11], 71), 0)
    w_key = draw_w_key(jax.random.fold_in(streams_of[11], 71), 0)
    value_weight = centred(streams_of[5], (MODEL_DIMENSION, KEY_VALUE_HEADS * HEAD_DIMENSION), MODEL_DIMENSION ** -0.5, 0.09375, ((0, 32),))
    w_out = centred(streams_of[6], (QUERY_HEADS * HEAD_DIMENSION, MODEL_DIMENSION), HEAD_DIMENSION ** -0.5, 0.5, ((0, 4), (1, 32)))
    routes_keys = jax.random.split(jax.random.fold_in(streams_of[7], 1), SEQUENCE_TOKENS // TOK_DEV)
    routes_turns = jax.random.permutation(jax.random.fold_in(streams_of[7], 3), SEQUENCE_TOKENS // TOK_DEV)
    routes = jax.vmap(lambda own, number: shared_out(jax.random.fold_in(streams_of[7], 2), own, number, TOK_DEV, EXPERTS, TOPK, CAP, 2))(routes_keys, routes_turns).reshape((SEQUENCE_TOKENS, TOPK))
    route_probs = jnp.clip(0.049804688 + 0.3486328 * jax.random.uniform(streams_of[8], (SEQUENCE_TOKENS, TOPK), jnp.float32) ** levels(streams_of[8], (SEQUENCE_TOKENS, TOPK), ((0, 32),), -0.2, 0.2), 0.049804688, 0.3984375).astype(jnp.bfloat16)
    w_gate_up = centred(streams_of[9], (EXPERTS, MODEL_DIMENSION, 2 * FFW), MODEL_DIMENSION ** -0.5, 0.09375, ((0, 128),))
    w_down = centred(streams_of[10], (EXPERTS, FFW, MODEL_DIMENSION), FFW ** -0.5, 0.21875, ((0, 128),))
    return dict(tokens=tokens, attn_gain=attn_gain, ffn_gain=ffn_gain, w_query=w_query, w_key=w_key, value_weight=value_weight, w_out=w_out, routes=routes, route_probs=route_probs, w_gate_up=w_gate_up, w_down=w_down)


EPSILON = 1e-06

def rms_scale(row_data, gain):
    floats = row_data.astype(jnp.float32)
    mean_sq = lax.optimization_barrier(jnp.mean(floats * floats, axis=-1, keepdims=True))
    return (floats * lax.rsqrt(mean_sq + EPSILON) * gain).astype(jnp.bfloat16)

def head_attention(query_rows, key_rows, value_rows):
    block_size = math.gcd(SEQUENCE_TOKENS, 512)
    block_count = SEQUENCE_TOKENS // block_size
    key_float = key_rows.astype(jnp.float32)
    value_float = value_rows.astype(jnp.float32)
    positions = jnp.arange(SEQUENCE_TOKENS, dtype=jnp.int32)

    def one_block(block_index):
        block_start = block_index * block_size
        query_block = lax.dynamic_slice_in_dim(query_rows, block_start, block_size, 0).astype(jnp.float32)
        scores = jnp.dot(query_block, key_float.T, precision=lax.Precision.HIGHEST) * HEAD_DIMENSION ** (-0.5)
        query_pos = block_start + jnp.arange(block_size, dtype=jnp.int32)
        allowed = positions[None, :] <= query_pos[:, None]
        masked = jnp.where(allowed, scores, -jnp.inf)
        row_best = lax.optimization_barrier(jnp.max(masked, axis=1, keepdims=True))
        weights = jnp.where(allowed, jnp.exp(masked - row_best), 0.0)
        row_total = lax.optimization_barrier(jnp.sum(weights, axis=1, keepdims=True))
        rounded = lax.optimization_barrier(weights.astype(jnp.bfloat16)).astype(jnp.float32)
        mixed = jnp.dot(rounded, value_float, precision=lax.Precision.HIGHEST) / row_total
        return mixed.astype(jnp.bfloat16)
    return lax.map(one_block, jnp.arange(block_count, dtype=jnp.int32)).reshape(SEQUENCE_TOKENS, HEAD_DIMENSION)

def reference(tokens, attn_gain, ffn_gain, w_query, w_key, value_weight, w_out, routes, route_probs, w_gate_up, w_down):
    normed = rms_scale(tokens, attn_gain)
    query = jnp.dot(normed, w_query, preferred_element_type=jnp.float32).astype(jnp.bfloat16)
    key_projected = jnp.dot(normed, w_key, preferred_element_type=jnp.float32).astype(jnp.bfloat16)
    value_projected = jnp.dot(normed, value_weight, preferred_element_type=jnp.float32).astype(jnp.bfloat16)
    query_heads = query.reshape(SEQUENCE_TOKENS, QUERY_HEADS, HEAD_DIMENSION).transpose(1, 0, 2)
    heads_of_keys = key_projected.reshape(SEQUENCE_TOKENS, KEY_VALUE_HEADS, HEAD_DIMENSION).transpose(1, 0, 2)
    heads_of_values = value_projected.reshape(SEQUENCE_TOKENS, KEY_VALUE_HEADS, HEAD_DIMENSION).transpose(1, 0, 2)
    shared_portion = QUERY_HEADS // KEY_VALUE_HEADS

    def one_head(head_index):
        key_value_head = head_index // shared_portion
        return head_attention(query_heads[head_index], heads_of_keys[key_value_head], heads_of_values[key_value_head])
    attended = lax.map(one_head, jnp.arange(QUERY_HEADS, dtype=jnp.int32))
    attended = attended.transpose(1, 0, 2).reshape(SEQUENCE_TOKENS, QUERY_HEADS * HEAD_DIMENSION)
    group_width = QUERY_HEADS * HEAD_DIMENSION // N_GRP
    head_total = jnp.zeros((SEQUENCE_TOKENS, MODEL_DIMENSION), jnp.float32)
    for group_index in range(N_GRP):
        lower = group_index * group_width
        partial_value = jnp.dot(attended[:, lower:lower + group_width], w_out[lower:lower + group_width], preferred_element_type=jnp.float32).astype(jnp.bfloat16)
        head_total = head_total + partial_value.astype(jnp.float32)
    attn_branch = head_total.astype(jnp.bfloat16)
    resid = (tokens.astype(jnp.float32) + attn_branch.astype(jnp.float32)).astype(jnp.bfloat16)
    ffn_in = rms_scale(resid, ffn_gain)
    assign = TOK_DEV * TOPK
    flat_routes = routes.reshape(N_FSDP, assign).astype(jnp.int32)
    expert_ids = jnp.arange(EXPERTS, dtype=jnp.int32)
    expert_hits = (flat_routes[:, :, None] == expert_ids[None, None, :]).astype(jnp.int32)
    slot_ids = (lax.optimization_barrier(jnp.sum(jnp.cumsum(expert_hits, axis=1) * expert_hits, axis=2)) - 1).astype(jnp.int32)
    block_ids = jnp.broadcast_to(jnp.arange(N_FSDP, dtype=jnp.int32)[:, None], (N_FSDP, assign))
    token_ids = (block_ids * TOK_DEV + jnp.arange(assign, dtype=jnp.int32)[None, :] // TOPK).astype(jnp.int32)
    slot_place = (block_ids * CAP + slot_ids).astype(jnp.int32)
    slot_table = jnp.full((EXPERTS, N_FSDP * CAP), -1, jnp.int32)
    slot_table = slot_table.at[flat_routes.reshape(-1), slot_place.reshape(-1)].set(token_ids.reshape(-1))

    def one_expert(expert_index):
        token_rows = slot_table[expert_index]
        occupied = token_rows >= 0
        row_data = ffn_in[jnp.maximum(token_rows, 0)]
        gate_up = jnp.dot(row_data, w_gate_up[expert_index], preferred_element_type=jnp.float32)
        hidden = (jax.nn.silu(gate_up[:, :FFW]) * gate_up[:, FFW:]).astype(jnp.bfloat16)
        result = jnp.dot(hidden, w_down[expert_index], preferred_element_type=jnp.float32).astype(jnp.bfloat16)
        return jnp.where(occupied[:, None], result, jnp.zeros_like(result))
    expert_out = lax.map(one_expert, expert_ids)
    prob_blocks = route_probs.reshape(N_FSDP, TOK_DEV, TOPK).astype(jnp.float32)

    def mix_block(block_index):
        block_experts = flat_routes[block_index]
        picked = expert_out[block_experts, slot_place[block_index]]
        picked = picked.reshape(TOK_DEV, TOPK, MODEL_DIMENSION).astype(jnp.float32)
        owner_group = block_experts.reshape(TOK_DEV, TOPK) // N_FSDP
        prob_block = prob_blocks[block_index]
        mix_total = jnp.zeros((TOK_DEV, MODEL_DIMENSION), jnp.float32)
        for group_index in range(N_GRP):
            weight = jnp.where(owner_group == group_index, prob_block, 0.0)
            partial_value = jnp.einsum('tk,tkd->td', weight, picked, precision=lax.Precision.HIGHEST).astype(jnp.bfloat16)
            mix_total = mix_total + partial_value.astype(jnp.float32)
        return mix_total
    expert_mix = lax.map(mix_block, jnp.arange(N_FSDP, dtype=jnp.int32)).reshape(SEQUENCE_TOKENS, MODEL_DIMENSION)
    layer_out = (resid.astype(jnp.float32) + expert_mix).astype(jnp.bfloat16)
    return (attn_branch, layer_out)
```

```python
import jax
import jax.numpy as jnp
from jax import lax
from jax.sharding import PartitionSpec as P

KEY_VALUE_HEADS = 2
HEAD_DIMENSION = 128
FFW = 768


EPSILON = 1e-06
FLOOR_SCORE = -1e30


def rms_scale(row_data, gain):
    floats = row_data.astype(jnp.float32)
    mean_sq = jnp.mean(floats * floats, axis=-1, keepdims=True)
    return (floats * lax.rsqrt(mean_sq + EPSILON) * gain).astype(jnp.bfloat16)


def attend_block(state, query_bf, key_block, value_block, key_start, positions):
    row_best, row_total, weighted = state
    scores = jnp.einsum(
        "thd,kd->thk", query_bf, key_block, preferred_element_type=jnp.float32
    ) * HEAD_DIMENSION ** (-0.5)
    key_pos = key_start + jnp.arange(key_block.shape[0], dtype=jnp.int32)
    allowed = (key_pos[None, :] <= positions[:, None])[:, None, :]
    masked = jnp.where(allowed, scores, FLOOR_SCORE)
    new_best = jnp.maximum(row_best, jnp.max(masked, axis=2))
    weights = jnp.where(allowed, jnp.exp(masked - new_best[:, :, None]), 0.0)
    rescale = jnp.exp(row_best - new_best)
    row_total = row_total * rescale + jnp.sum(weights, axis=2)
    weighted = weighted * rescale[:, :, None] + jnp.einsum(
        "thk,kd->thd", weights.astype(jnp.bfloat16), value_block, preferred_element_type=jnp.float32
    )
    return (new_best, row_total, weighted)


def on_device(
    tokens,
    attn_gain,
    ffn_gain,
    w_query,
    w_key,
    value_weight,
    w_out,
    routes,
    route_probs,
    w_gate_up,
    w_down,
):
    head_groups = lax.axis_size("grp")
    fsdp_size = lax.axis_size("fsdp")
    current_group = lax.axis_index("grp")
    my_rank = lax.axis_index("fsdp")
    tok_rows = tokens.shape[0]
    model_width = tokens.shape[1]
    head_width = w_query.shape[1]
    group_heads = head_width // HEAD_DIMENSION
    key_value_head = current_group * KEY_VALUE_HEADS // head_groups
    normed = rms_scale(tokens, attn_gain)
    key_cols = lax.dynamic_slice_in_dim(w_key, key_value_head * HEAD_DIMENSION, HEAD_DIMENSION, 1)
    value_cols = lax.dynamic_slice_in_dim(
        value_weight, key_value_head * HEAD_DIMENSION, HEAD_DIMENSION, 1
    )
    query = jnp.dot(
        normed,
        lax.all_gather(w_query, "fsdp", axis=0, tiled=True),
        preferred_element_type=jnp.float32,
    )
    key_local = jnp.dot(
        normed,
        lax.all_gather(key_cols, "fsdp", axis=0, tiled=True),
        preferred_element_type=jnp.float32,
    )
    value_local = jnp.dot(
        normed,
        lax.all_gather(value_cols, "fsdp", axis=0, tiled=True),
        preferred_element_type=jnp.float32,
    )
    query_bf = query.astype(jnp.bfloat16).reshape(tok_rows, group_heads, HEAD_DIMENSION)
    key_local = key_local.astype(jnp.bfloat16)
    value_local = value_local.astype(jnp.bfloat16)
    first_row = my_rank * tok_rows
    positions = first_row + jnp.arange(tok_rows, dtype=jnp.int32)
    last_query = first_row + tok_rows - 1
    attend_init = (
        jnp.full((tok_rows, group_heads), FLOOR_SCORE, jnp.float32),
        jnp.zeros((tok_rows, group_heads), jnp.float32),
        jnp.zeros((tok_rows, group_heads, HEAD_DIMENSION), jnp.float32),
    )
    state = attend_init
    key_rows = lax.all_gather(key_local, "fsdp", axis=0, tiled=True)
    value_rows = lax.all_gather(value_local, "fsdp", axis=0, tiled=True)
    row_count = key_rows.shape[0]
    key_span = 1024

    def visit(running, step_index):
        block_start = step_index * key_span
        key_block = lax.dynamic_slice_in_dim(key_rows, block_start, key_span, 0)
        value_block = lax.dynamic_slice_in_dim(value_rows, block_start, key_span, 0)
        needed = block_start <= last_query
        running = lax.cond(
            needed,
            lambda inner: attend_block(
                inner, query_bf, key_block, value_block, block_start, positions
            ),
            lambda inner: inner,
            running,
        )
        return (running, None)

    state, _ = lax.scan(visit, state, jnp.arange(row_count // key_span, dtype=jnp.int32))
    row_best, row_total, weighted = state
    attended = (weighted / row_total[:, :, None]).astype(jnp.bfloat16).reshape(tok_rows, head_width)
    head_part = jnp.dot(
        attended,
        lax.all_gather(w_out, "fsdp", axis=1, tiled=True),
        preferred_element_type=jnp.float32,
    ).astype(jnp.bfloat16)
    attn_branch = lax.psum(head_part.astype(jnp.float32).astype(jnp.bfloat16), "grp")
    resid = (tokens.astype(jnp.float32) + attn_branch.astype(jnp.float32)).astype(jnp.bfloat16)
    ffn_in = rms_scale(resid, ffn_gain)
    top_count = routes.shape[1]
    experts_all = head_groups * fsdp_size
    capacity = max(2, 3 * tok_rows * top_count // (2 * experts_all))
    group_rows = fsdp_size * capacity
    group_experts = fsdp_size
    expert_ids = current_group * group_experts + jnp.arange(group_experts, dtype=jnp.int32)
    named = routes[:, :, None] == expert_ids[None, None, :]
    hits = jnp.any(named, axis=1)
    token_ids = jnp.arange(tok_rows, dtype=jnp.int32)
    earlier = (token_ids[None, :] < token_ids[:, None]).astype(jnp.bfloat16)
    rank = jnp.dot(earlier, hits.astype(jnp.bfloat16), preferred_element_type=jnp.float32)
    code = jnp.where(hits, rank, -1.0).astype(jnp.bfloat16)
    row_ids = jnp.arange(group_rows, dtype=jnp.int32)
    spread = (
        row_ids[None, :] // capacity == jnp.arange(group_experts, dtype=jnp.int32)[:, None]
    ).astype(jnp.bfloat16)
    code_rows = jnp.dot(code, spread, preferred_element_type=jnp.float32)
    slot_match = code_rows == (row_ids % capacity).astype(jnp.float32)[None, :]
    chosen = slot_match.astype(jnp.bfloat16)
    outbound = (
        jnp.einsum("tr,td->rd", chosen, ffn_in, preferred_element_type=jnp.float32)
        .astype(jnp.bfloat16)
        .reshape(fsdp_size, capacity, model_width)
    )
    gate_proj = w_gate_up[0]
    down_proj = w_down[0]
    col_width = model_width // head_groups
    arrived = lax.all_to_all(outbound, "fsdp", split_axis=0, concat_axis=0, tiled=True)
    slot_count = arrived.shape[1]
    arrived_rows = arrived.reshape(-1, model_width)
    gate_up = jnp.dot(arrived_rows, gate_proj, preferred_element_type=jnp.float32)
    hidden = (jax.nn.silu(gate_up[:, :FFW]) * gate_up[:, FFW:]).astype(jnp.bfloat16)
    result = jnp.dot(hidden, down_proj, preferred_element_type=jnp.float32).astype(jnp.bfloat16)
    returned = lax.all_to_all(
        result.reshape(fsdp_size, slot_count, model_width),
        "fsdp",
        split_axis=0,
        concat_axis=0,
        tiled=True,
    )
    named_probs = jnp.sum(jnp.where(named, route_probs[:, :, None], 0.0), axis=1)
    prob_rows = jnp.dot(
        named_probs.astype(jnp.bfloat16), spread, preferred_element_type=jnp.float32
    )
    mixing = jnp.where(slot_match, prob_rows, 0.0).astype(jnp.bfloat16)
    group_part = jnp.dot(
        mixing, returned.reshape(group_rows, model_width), preferred_element_type=jnp.float32
    ).astype(jnp.bfloat16)
    expert_mix = lax.psum_scatter(
        group_part.astype(jnp.float32).astype(jnp.bfloat16), "grp", scatter_dimension=1, tiled=True
    ).astype(jnp.float32)
    own_cols = lax.dynamic_slice_in_dim(resid, current_group * col_width, col_width, 1)
    layer_out = (own_cols.astype(jnp.float32) + expert_mix).astype(jnp.bfloat16)
    return (attn_branch, layer_out)


def solution(mesh):
    placed = (
        P("fsdp", None),
        P(),
        P(),
        P("fsdp", "grp"),
        P("fsdp", None),
        P("fsdp", None),
        P("grp", "fsdp"),
        P("fsdp", None),
        P("fsdp", None),
        P(("grp", "fsdp"), None, None),
        P(("grp", "fsdp"), None, None),
    )
    return jax.shard_map(
        on_device,
        mesh=mesh,
        in_specs=placed,
        out_specs=(P("fsdp", None), P("fsdp", "grp")),
        check_vma=False,
    )
```

```python
import functools

import jax
import jax.numpy as jnp
from jax import lax
from jax.experimental import pallas as pl
from jax.experimental.pallas import tpu as pltpu
from jax.sharding import PartitionSpec as P

KEY_VALUE_HEADS = 2
HEAD_DIMENSION = 128
FFW = 768


EPSILON = 1e-06
FLOOR_SCORE = -1e30
LOG2_E = 1.4426950408889634
KEY_SPAN = 1024
QUERY_TILE = 128
HIDDEN_TILE = 256
NORM_TILE = 64


def rms_scale(row_data, gain):
    floats = row_data.astype(jnp.float32)
    mean_sq = jnp.mean(floats * floats, axis=-1, keepdims=True)
    return (floats * lax.rsqrt(mean_sq + EPSILON) * gain).astype(jnp.bfloat16)


def attend_kernel(rank_ref, query_ref, pairs_ref, out_ref, best, weighted, *, span, heads):
    rank = rank_ref[0]
    rows = query_ref.shape[0]
    factor = HEAD_DIMENSION**-0.5 * LOG2_E
    best[...] = jnp.full_like(best, FLOOR_SCORE)
    weighted[...] = jnp.zeros_like(weighted)

    def step(index, masked):
        start = pl.multiple_of(index * span, span)
        keys = pairs_ref[pl.ds(start, span), :HEAD_DIMENSION]
        values = pairs_ref[pl.ds(start, span), HEAD_DIMENSION:]
        values = jnp.concatenate([values, jnp.ones_like(values)], axis=1)
        for head in range(heads):
            for row in range(0, rows, QUERY_TILE):
                tile = slice(row, row + QUERY_TILE)
                query = query_ref[tile, head * HEAD_DIMENSION : (head + 1) * HEAD_DIMENSION]
                scores = lax.dot_general(
                    query, keys, (((1,), (1,)), ((), ())), preferred_element_type=jnp.float32
                )
                if masked:
                    key_pos = lax.broadcasted_iota(jnp.int32, scores.shape, 1) + start
                    query_pos = lax.broadcasted_iota(jnp.int32, scores.shape, 0) + (
                        rank * rows + row
                    )
                    scores = jnp.where(key_pos <= query_pos, scores, FLOOR_SCORE)
                old = best[head, tile]
                new = jnp.maximum(old, jnp.max(scores, axis=1, keepdims=True))
                weights = jnp.exp2((scores - jnp.tile(new, (1, span // HEAD_DIMENSION))) * factor)
                rescale = jnp.exp2((old - new) * factor)
                best[head, tile] = new
                weighted[head, tile] = weighted[head, tile] * jnp.tile(rescale, (1, 2)) + jnp.dot(
                    weights.astype(jnp.bfloat16), values, preferred_element_type=jnp.float32
                )

    full = rank * rows // span

    def visit(index, carry):
        step(index, False)
        return carry

    lax.fori_loop(0, full, visit, 0)
    step(full, True)
    for head in range(heads):
        out_ref[:, head * HEAD_DIMENSION : (head + 1) * HEAD_DIMENSION] = (
            weighted[head, :, :HEAD_DIMENSION] / weighted[head, :, HEAD_DIMENSION:]
        ).astype(out_ref.dtype)


def attend(rank, query, pairs):
    rows, width = query.shape
    heads = width // HEAD_DIMENSION
    keys = pairs.shape[0]
    span = min(KEY_SPAN, keys)
    return pl.pallas_call(
        functools.partial(attend_kernel, span=span, heads=heads),
        out_shape=jax.ShapeDtypeStruct(query.shape, query.dtype),
        in_specs=[
            pl.BlockSpec(memory_space=pltpu.SMEM),
            pl.BlockSpec(memory_space=pltpu.VMEM),
            pl.BlockSpec(memory_space=pltpu.VMEM),
        ],
        out_specs=pl.BlockSpec(memory_space=pltpu.VMEM),
        scratch_shapes=[
            pltpu.VMEM((heads, rows, HEAD_DIMENSION), jnp.float32),
            pltpu.VMEM((heads, rows, 2 * HEAD_DIMENSION), jnp.float32),
        ],
        compiler_params=pltpu.CompilerParams(vmem_limit_bytes=40 * 2**20),
        cost_estimate=pl.CostEstimate(
            flops=4 * rows * keys * width,
            bytes_accessed=4 * rows * width + 4 * keys * HEAD_DIMENSION,
            transcendentals=rows * keys * heads,
        ),
    )(rank, query, pairs)


def expert_kernel(rows_ref, gain_ref, gate_ref, up_ref, down_ref, out_ref, normed, hidden, *, wide):
    step = pl.program_id(0)
    parts, rows, width = rows_ref.shape

    @pl.when(step == 0)
    def _():
        def scale_rows(index, carry):
            tile = pl.ds(pl.multiple_of(index * NORM_TILE, NORM_TILE), NORM_TILE)
            floats = [rows_ref[part, tile, :].astype(jnp.float32) for part in range(parts)]
            squares = sum(values * values for values in floats)
            mean_sq = jnp.sum(squares, axis=1, keepdims=True) / (parts * width)
            scale = lax.rsqrt(mean_sq + EPSILON)
            for part in range(parts):
                normed[part, tile, :] = (floats[part] * scale * gain_ref[part]).astype(jnp.bfloat16)
            return carry

        lax.fori_loop(0, rows // NORM_TILE, scale_rows, 0)

    @pl.when(step < wide)
    def _():
        def project(weight_ref):
            return sum(
                jnp.dot(
                    normed[part],
                    weight_ref[0, part * width : (part + 1) * width, :],
                    preferred_element_type=jnp.float32,
                )
                for part in range(parts)
            )

        hidden[step] = (jax.nn.silu(project(gate_ref)) * project(up_ref)).astype(jnp.bfloat16)

    @pl.when(step >= wide)
    def _():
        out_ref[0] = sum(
            jnp.dot(
                hidden[tile],
                down_ref[0, tile * HIDDEN_TILE : (tile + 1) * HIDDEN_TILE, :],
                preferred_element_type=jnp.float32,
            )
            for tile in range(wide)
        ).astype(out_ref.dtype)


def run_expert(arrived, gain, w_gate_up, w_down):
    parts, rows, width = arrived.shape
    model_width = parts * width
    wide = FFW // HIDDEN_TILE
    return pl.pallas_call(
        functools.partial(expert_kernel, wide=wide),
        grid=(wide + parts,),
        out_shape=jax.ShapeDtypeStruct(arrived.shape, arrived.dtype),
        in_specs=[
            pl.BlockSpec((parts, rows, width), lambda i: (0, 0, 0)),
            pl.BlockSpec((parts, 1, width), lambda i: (0, 0, 0)),
            pl.BlockSpec((1, model_width, HIDDEN_TILE), lambda i: (0, 0, jnp.minimum(i, wide - 1))),
            pl.BlockSpec(
                (1, model_width, HIDDEN_TILE), lambda i: (0, 0, wide + jnp.minimum(i, wide - 1))
            ),
            pl.BlockSpec((1, FFW, width), lambda i: (0, 0, jnp.maximum(i - wide, 0))),
        ],
        out_specs=pl.BlockSpec((1, rows, width), lambda i: (jnp.maximum(i - wide, 0), 0, 0)),
        scratch_shapes=[
            pltpu.VMEM((parts, rows, width), jnp.bfloat16),
            pltpu.VMEM((wide, rows, HIDDEN_TILE), jnp.bfloat16),
        ],
        compiler_params=pltpu.CompilerParams(vmem_limit_bytes=54 * 2**20),
        cost_estimate=pl.CostEstimate(
            flops=6 * rows * model_width * FFW,
            bytes_accessed=4 * rows * model_width + 6 * model_width * FFW,
            transcendentals=rows * FFW,
        ),
    )(arrived, gain.reshape(parts, 1, width), w_gate_up, w_gate_up, w_down)


def on_device(
    tokens,
    attn_gain,
    ffn_gain,
    w_query,
    w_key,
    value_weight,
    w_out,
    routes,
    route_probs,
    w_gate_up,
    w_down,
):
    head_groups = lax.axis_size("grp")
    fsdp_size = lax.axis_size("fsdp")
    current_group = lax.axis_index("grp")
    my_rank = lax.axis_index("fsdp")
    tok_rows, model_width = tokens.shape
    head_width = w_query.shape[1]
    col_width = model_width // head_groups
    key_value_head = current_group * KEY_VALUE_HEADS // head_groups
    key_cols = lax.dynamic_slice_in_dim(w_key, key_value_head * HEAD_DIMENSION, HEAD_DIMENSION, 1)
    value_cols = lax.dynamic_slice_in_dim(
        value_weight, key_value_head * HEAD_DIMENSION, HEAD_DIMENSION, 1
    )
    w_joint = lax.all_gather(
        jnp.concatenate([w_query, key_cols, value_cols], axis=1), "fsdp", axis=0, tiled=True
    )
    normed = rms_scale(tokens, attn_gain)
    joint = jnp.dot(normed, w_joint, preferred_element_type=jnp.float32).astype(jnp.bfloat16)
    pairs = lax.all_gather(joint[:, head_width:], "fsdp", axis=0, tiled=True)
    attended = attend(my_rank.astype(jnp.int32).reshape(1), joint[:, :head_width], pairs)
    head_part = jnp.dot(
        attended,
        lax.all_gather(w_out, "fsdp", axis=1, tiled=True),
        preferred_element_type=jnp.float32,
    ).astype(jnp.bfloat16)
    branch_cols = lax.psum_scatter(head_part, "grp", scatter_dimension=1, tiled=True)
    attn_branch = lax.all_gather(branch_cols, "grp", axis=1, tiled=True)
    own_cols = lax.dynamic_slice_in_dim(tokens, current_group * col_width, col_width, 1)
    resid = (own_cols.astype(jnp.float32) + branch_cols.astype(jnp.float32)).astype(jnp.bfloat16)

    top_count = routes.shape[1]
    experts_all = head_groups * fsdp_size
    capacity = max(2, 3 * tok_rows * top_count // (2 * experts_all))
    slots = experts_all * capacity
    expert_ids = jnp.arange(experts_all, dtype=jnp.int32)
    named = routes[:, :, None] == expert_ids[None, None, :]
    hits = jnp.any(named, axis=1)
    token_ids = jnp.arange(tok_rows, dtype=jnp.int32)
    earlier = (token_ids[None, :] < token_ids[:, None]).astype(jnp.bfloat16)
    rank = jnp.dot(earlier, hits.astype(jnp.bfloat16), preferred_element_type=jnp.float32)
    code = jnp.where(hits, rank, -1.0).astype(jnp.bfloat16)
    slot_list = jnp.arange(slots, dtype=jnp.int32)
    spread = (slot_list[None, :] // capacity == expert_ids[:, None]).astype(jnp.bfloat16)
    code_slots = jnp.dot(code, spread, preferred_element_type=jnp.float32)
    slot_match = code_slots == (slot_list % capacity).astype(jnp.float32)[None, :]
    chosen = slot_match.astype(jnp.bfloat16)
    named_probs = jnp.sum(jnp.where(named, route_probs[:, :, None], 0.0), axis=1)
    prob_slots = jnp.dot(
        named_probs.astype(jnp.bfloat16), spread, preferred_element_type=jnp.float32
    )
    mixing = jnp.where(slot_match, prob_slots, 0.0).astype(jnp.bfloat16)

    outbound = lax.dot_general(
        chosen, resid, (((0,), (0,)), ((), ())), preferred_element_type=jnp.float32
    ).astype(jnp.bfloat16)
    arrived = lax.all_to_all(
        outbound.reshape(experts_all, capacity, col_width),
        ("grp", "fsdp"),
        split_axis=0,
        concat_axis=0,
        tiled=True,
    )
    result = run_expert(
        arrived.reshape(head_groups, fsdp_size * capacity, col_width), ffn_gain, w_gate_up, w_down
    )
    returned = lax.all_to_all(
        result.reshape(experts_all, capacity, col_width),
        ("grp", "fsdp"),
        split_axis=0,
        concat_axis=0,
        tiled=True,
    )
    expert_mix = jnp.dot(
        mixing, returned.reshape(slots, col_width), preferred_element_type=jnp.float32
    )
    layer_out = (resid.astype(jnp.float32) + expert_mix).astype(jnp.bfloat16)
    return (attn_branch, layer_out)


def solution(mesh):
    placed = (
        P("fsdp", None),
        P(),
        P(),
        P("fsdp", "grp"),
        P("fsdp", None),
        P("fsdp", None),
        P("grp", "fsdp"),
        P("fsdp", None),
        P("fsdp", None),
        P(("grp", "fsdp"), None, None),
        P(("grp", "fsdp"), None, None),
    )
    return jax.shard_map(
        on_device,
        mesh=mesh,
        in_specs=placed,
        out_specs=(P("fsdp", None), P("fsdp", "grp")),
        check_vma=False,
    )
```

```python
import functools

import jax
import jax.numpy as jnp
from jax import lax
from jax.experimental import pallas as pl
from jax.experimental.pallas import tpu as pltpu
from jax.sharding import PartitionSpec as P

KEY_VALUE_HEADS = 2
HEAD_DIMENSION = 128
FFW = 768


EPSILON = 1e-06
FLOOR_SCORE = -1e30
LOG2_E = 1.4426950408889634
SIDE = 4
QUERY_TILE = 128
HIDDEN_TILE = 256
NORM_TILE = 64


def rms_scale(row_data, gain):
    floats = row_data.astype(jnp.float32)
    mean_sq = jnp.mean(floats * floats, axis=-1, keepdims=True)
    return (floats * lax.rsqrt(mean_sq + EPSILON) * gain).astype(jnp.bfloat16)


def to_other_core(rows):
    return lax.ppermute(rows, "fsdp", [(i, i ^ 1) for i in range(2 * SIDE * SIDE)])


def from_group(rows, shift):
    return lax.ppermute(rows, "grp", [((i + shift) % SIDE, i) for i in range(SIDE)])


def from_chips(rows):
    chips = SIDE * SIDE
    parts = lax.all_to_all(
        jnp.broadcast_to(rows[None], (chips, *rows.shape)),
        "fsdp",
        split_axis=0,
        concat_axis=0,
        axis_index_groups=[[2 * chip + core for chip in range(chips)] for core in range(2)],
        tiled=True,
    )
    return parts.reshape(chips * rows.shape[0], rows.shape[1])


def by_core(core, mine, other):
    return jnp.concatenate(
        [jnp.where(core == 0, mine, other), jnp.where(core == 0, other, mine)], axis=0
    )


def attend_kernel(
    rank_ref,
    query_ref,
    mine_ref,
    other_ref,
    out_ref,
    best,
    weighted,
    *,
    heads,
    first_head,
):
    rank = rank_ref[0]
    rows = query_ref.shape[0]
    span = 4 * rows
    core = rank % 2
    factor = HEAD_DIMENSION**-0.5 * LOG2_E
    best[...] = jnp.full_like(best, FLOOR_SCORE)
    weighted[...] = jnp.zeros_like(weighted)

    def step(index, masked):
        start = pl.multiple_of(index * span, span)
        mine = mine_ref[pl.ds(start, span), :]
        other = other_ref[pl.ds(start, span), :]
        keys = jnp.where(core == 0, mine, other)
        values = jnp.where(core == 0, other, mine)
        values = jnp.concatenate([values, jnp.ones_like(values)], axis=1)
        for head in range(heads):
            cols = slice((first_head + head) * HEAD_DIMENSION, (first_head + head + 1) * HEAD_DIMENSION)
            for row in range(0, rows, QUERY_TILE):
                tile = slice(row, row + QUERY_TILE)
                scores = lax.dot_general(
                    query_ref[tile, cols],
                    keys,
                    (((1,), (1,)), ((), ())),
                    preferred_element_type=jnp.float32,
                )
                if masked:
                    key_pos = lax.broadcasted_iota(jnp.int32, scores.shape, 1) + start
                    query_pos = lax.broadcasted_iota(jnp.int32, scores.shape, 0) + (
                        rank * rows + row
                    )
                    scores = jnp.where(key_pos <= query_pos, scores, FLOOR_SCORE)
                old = best[head, tile]
                new = jnp.maximum(old, jnp.max(scores, axis=1, keepdims=True))
                weights = jnp.exp2((scores - jnp.tile(new, (1, span // HEAD_DIMENSION))) * factor)
                rescale = jnp.exp2((old - new) * factor)
                best[head, tile] = new
                weighted[head, tile] = weighted[head, tile] * jnp.tile(rescale, (1, 2)) + jnp.dot(
                    weights.astype(jnp.bfloat16), values, preferred_element_type=jnp.float32
                )

    full = rank * rows // span

    def visit(index, carry):
        step(index, False)
        return carry

    lax.fori_loop(0, full, visit, 0)
    step(full, True)
    for head in range(heads):
        out_ref[:, head * HEAD_DIMENSION : (head + 1) * HEAD_DIMENSION] = (
            weighted[head, :, :HEAD_DIMENSION] / weighted[head, :, HEAD_DIMENSION:]
        ).astype(out_ref.dtype)


def attend(rank, query, gathered, first_head, heads):
    rows = query.shape[0]
    width = heads * HEAD_DIMENSION
    keys = gathered[0].shape[0]
    return pl.pallas_call(
        functools.partial(attend_kernel, heads=heads, first_head=first_head),
        out_shape=jax.ShapeDtypeStruct((rows, width), query.dtype),
        in_specs=[pl.BlockSpec(memory_space=pltpu.SMEM)]
        + [pl.BlockSpec(memory_space=pltpu.VMEM)] * (1 + len(gathered)),
        out_specs=pl.BlockSpec(memory_space=pltpu.VMEM),
        scratch_shapes=[
            pltpu.VMEM((heads, rows, HEAD_DIMENSION), jnp.float32),
            pltpu.VMEM((heads, rows, 2 * HEAD_DIMENSION), jnp.float32),
        ],
        compiler_params=pltpu.CompilerParams(vmem_limit_bytes=32 * 2**20),
        cost_estimate=pl.CostEstimate(
            flops=8 * rows * keys * width,
            bytes_accessed=4 * rows * width + 4 * keys * HEAD_DIMENSION,
            transcendentals=rows * keys * heads,
        ),
    )(rank, query, *gathered)


def project_kernel(group_ref, *refs):
    *part_refs, weight_ref, out_ref, total = refs
    step = pl.program_id(0)
    groups = len(part_refs) // 2
    half = part_refs[0].shape[1]
    weights = jnp.concatenate([weight_ref[0, i] for i in range(weight_ref.shape[1])], axis=1)

    def product(index):
        return jnp.dot(
            part_refs[2 * index][...], weights[:half], preferred_element_type=jnp.float32
        ) + jnp.dot(
            part_refs[2 * index + 1][...], weights[half:], preferred_element_type=jnp.float32
        )

    for index in range(groups):

        @pl.when(step == index)
        def _(index=index):
            if index == 0:
                total[...] = product(index)
            elif index < groups - 1:
                total[...] += product(index)
            else:
                out_ref[...] = (total[...] + product(index)).astype(out_ref.dtype)


def project(group, parts, weights):
    rows, half = parts[0].shape
    groups, blocks, depth, block_cols = weights.shape
    cols = blocks * block_cols
    return pl.pallas_call(
        project_kernel,
        grid_spec=pltpu.PrefetchScalarGridSpec(
            num_scalar_prefetch=1,
            grid=(groups,),
            in_specs=[pl.BlockSpec((rows, half), lambda i, group: (0, 0))] * len(parts)
            + [
                pl.BlockSpec(
                    (1, blocks, depth, block_cols),
                    lambda i, group: ((group[0] + i) % groups, 0, 0, 0),
                ),
            ],
            out_specs=pl.BlockSpec((rows, cols), lambda i, group: (0, 0)),
            scratch_shapes=[pltpu.VMEM((rows, cols), jnp.float32)],
        ),
        out_shape=jax.ShapeDtypeStruct((rows, cols), jnp.bfloat16),
        compiler_params=pltpu.CompilerParams(vmem_limit_bytes=32 * 2**20),
        cost_estimate=pl.CostEstimate(
            flops=2 * groups * rows * depth * cols,
            bytes_accessed=2 * groups * depth * (rows + cols),
            transcendentals=0,
        ),
    )(group, *parts, weights)


def expert_kernel(rows_ref, gain_ref, gate_ref, up_ref, down_ref, out_ref, normed, hidden, *, wide):
    step = pl.program_id(0)
    parts, rows, width = rows_ref.shape

    @pl.when(step == 0)
    def _():
        def scale_rows(index, carry):
            tile = pl.ds(pl.multiple_of(index * NORM_TILE, NORM_TILE), NORM_TILE)
            floats = [rows_ref[part, tile, :].astype(jnp.float32) for part in range(parts)]
            squares = sum(values * values for values in floats)
            mean_sq = jnp.sum(squares, axis=1, keepdims=True) / (parts * width)
            scale = lax.rsqrt(mean_sq + EPSILON)
            for part in range(parts):
                normed[part, tile, :] = (floats[part] * scale * gain_ref[part]).astype(jnp.bfloat16)
            return carry

        lax.fori_loop(0, rows // NORM_TILE, scale_rows, 0)

    @pl.when(step < wide)
    def _():
        def project(weight_ref):
            return sum(
                jnp.dot(
                    normed[part],
                    weight_ref[0, part * width : (part + 1) * width, :],
                    preferred_element_type=jnp.float32,
                )
                for part in range(parts)
            )

        hidden[step] = (jax.nn.silu(project(gate_ref)) * project(up_ref)).astype(jnp.bfloat16)

    @pl.when(step >= wide)
    def _():
        out_ref[0] = sum(
            jnp.dot(
                hidden[tile],
                down_ref[0, tile * HIDDEN_TILE : (tile + 1) * HIDDEN_TILE, :],
                preferred_element_type=jnp.float32,
            )
            for tile in range(wide)
        ).astype(out_ref.dtype)


def run_expert(arrived, gain, w_gate_up, w_down):
    parts, rows, width = arrived.shape
    model_width = parts * width
    wide = FFW // HIDDEN_TILE
    return pl.pallas_call(
        functools.partial(expert_kernel, wide=wide),
        grid=(wide + parts,),
        out_shape=jax.ShapeDtypeStruct(arrived.shape, arrived.dtype),
        in_specs=[
            pl.BlockSpec((parts, rows, width), lambda i: (0, 0, 0)),
            pl.BlockSpec((parts, 1, width), lambda i: (0, 0, 0)),
            pl.BlockSpec((1, model_width, HIDDEN_TILE), lambda i: (0, 0, jnp.minimum(i, wide - 1))),
            pl.BlockSpec(
                (1, model_width, HIDDEN_TILE), lambda i: (0, 0, wide + jnp.minimum(i, wide - 1))
            ),
            pl.BlockSpec((1, FFW, width), lambda i: (0, 0, jnp.maximum(i - wide, 0))),
        ],
        out_specs=pl.BlockSpec((1, rows, width), lambda i: (jnp.maximum(i - wide, 0), 0, 0)),
        scratch_shapes=[
            pltpu.VMEM((parts, rows, width), jnp.bfloat16),
            pltpu.VMEM((wide, rows, HIDDEN_TILE), jnp.bfloat16),
        ],
        compiler_params=pltpu.CompilerParams(vmem_limit_bytes=54 * 2**20),
        cost_estimate=pl.CostEstimate(
            flops=6 * rows * model_width * FFW,
            bytes_accessed=4 * rows * model_width + 6 * model_width * FFW,
            transcendentals=rows * FFW,
        ),
    )(arrived, gain.reshape(parts, 1, width), w_gate_up, w_gate_up, w_down)


def on_device(
    tokens,
    attn_gain,
    ffn_gain,
    w_query,
    w_key,
    value_weight,
    w_out,
    routes,
    route_probs,
    w_gate_up,
    w_down,
):
    head_groups = lax.axis_size("grp")
    fsdp_size = lax.axis_size("fsdp")
    current_group = lax.axis_index("grp")
    my_rank = lax.axis_index("fsdp")
    tok_rows, model_width = tokens.shape
    head_width = w_query.shape[1]
    col_width = model_width // head_groups
    key_value_head = current_group * KEY_VALUE_HEADS // head_groups
    key_cols = lax.dynamic_slice_in_dim(w_key, key_value_head * HEAD_DIMENSION, HEAD_DIMENSION, 1)
    value_cols = lax.dynamic_slice_in_dim(
        value_weight, key_value_head * HEAD_DIMENSION, HEAD_DIMENSION, 1
    )
    core = my_rank % 2
    w_query_all = lax.all_gather(w_query, "fsdp", axis=0, tiled=True)
    normed = lax.optimization_barrier(rms_scale(tokens, attn_gain))
    normed_other = to_other_core(normed)
    w_own = jnp.where(core == 0, key_cols, value_cols)
    w_given = to_other_core(jnp.where(core == 0, value_cols, key_cols))
    w_pair, normed = lax.optimization_barrier((by_core(core, w_own, w_given), normed))
    w_kv = from_chips(w_pair)

    def project_kv(rows):
        return jnp.dot(rows, w_kv, preferred_element_type=jnp.float32).astype(jnp.bfloat16)

    kv_local = by_core(core, project_kv(normed), project_kv(normed_other))
    w_out_block, w_kv = lax.optimization_barrier((w_out, w_kv))
    w_turned = lax.ppermute(
        w_out_block,
        ("grp", "fsdp"),
        [
            (g * fsdp_size + f, f // 8 * fsdp_size + g * 8 + f % 8)
            for g in range(head_groups)
            for f in range(fsdp_size)
        ],
    )
    w_turned, kv_local = lax.optimization_barrier((w_turned, kv_local))
    w_out_all = lax.all_gather(w_turned, "fsdp", axis=0, tiled=True)
    kv_mine = from_chips(kv_local)
    gathered = (kv_mine, to_other_core(kv_mine))
    query = jnp.dot(normed, w_query_all, preferred_element_type=jnp.float32).astype(jnp.bfloat16)
    rank_array = my_rank.astype(jnp.int32).reshape(1)
    half_heads = head_width // HEAD_DIMENSION // 2
    first = attend(rank_array, query, gathered, 0, half_heads)
    first_all = [first] + [from_group(first, shift) for shift in range(1, head_groups)]
    second = attend(rank_array, query, gathered, half_heads, half_heads)
    second_all = [second] + [from_group(second, shift) for shift in range(1, head_groups)]
    branch_cols = project(
        current_group.astype(jnp.int32).reshape(1),
        [part for pair in zip(first_all, second_all) for part in pair],
        w_out_all.reshape(head_groups, fsdp_size // head_groups, *w_out.shape),
    )
    own_cols = lax.dynamic_slice_in_dim(tokens, current_group * col_width, col_width, 1)
    resid = (own_cols.astype(jnp.float32) + branch_cols.astype(jnp.float32)).astype(jnp.bfloat16)

    top_count = routes.shape[1]
    experts_all = head_groups * fsdp_size
    capacity = max(2, 3 * tok_rows * top_count // (2 * experts_all))
    slots = experts_all * capacity
    expert_ids = jnp.arange(experts_all, dtype=jnp.int32)
    named = routes[:, :, None] == expert_ids[None, None, :]
    hits = jnp.any(named, axis=1)
    token_ids = jnp.arange(tok_rows, dtype=jnp.int32)
    earlier = (token_ids[None, :] < token_ids[:, None]).astype(jnp.bfloat16)
    rank = jnp.dot(earlier, hits.astype(jnp.bfloat16), preferred_element_type=jnp.float32)
    code = jnp.where(hits, rank, -1.0).astype(jnp.bfloat16)
    slot_list = jnp.arange(slots, dtype=jnp.int32)
    spread = (slot_list[None, :] // capacity == expert_ids[:, None]).astype(jnp.bfloat16)
    code_slots = jnp.dot(code, spread, preferred_element_type=jnp.float32)
    slot_match = code_slots == (slot_list % capacity).astype(jnp.float32)[None, :]
    chosen = slot_match.astype(jnp.bfloat16)
    named_probs = jnp.sum(jnp.where(named, route_probs[:, :, None], 0.0), axis=1)
    prob_slots = jnp.dot(
        named_probs.astype(jnp.bfloat16), spread, preferred_element_type=jnp.float32
    )
    mixing = jnp.where(slot_match, prob_slots, 0.0).astype(jnp.bfloat16)

    outbound = lax.dot_general(
        chosen, resid, (((0,), (0,)), ((), ())), preferred_element_type=jnp.float32
    ).astype(jnp.bfloat16)
    arrived = lax.all_to_all(
        outbound.reshape(experts_all, capacity, col_width),
        ("grp", "fsdp"),
        split_axis=0,
        concat_axis=0,
        tiled=True,
    )
    arrived, branch_cols = lax.optimization_barrier((arrived, branch_cols))
    attn_branch = lax.all_gather(branch_cols, "grp", axis=1, tiled=True)
    result = run_expert(
        arrived.reshape(head_groups, fsdp_size * capacity, col_width), ffn_gain, w_gate_up, w_down
    )
    result, attn_branch = lax.optimization_barrier((result, attn_branch))
    returned = lax.all_to_all(
        result.reshape(experts_all, capacity, col_width),
        ("grp", "fsdp"),
        split_axis=0,
        concat_axis=0,
        tiled=True,
    )
    expert_mix = jnp.dot(
        mixing, returned.reshape(slots, col_width), preferred_element_type=jnp.float32
    )
    layer_out = (resid.astype(jnp.float32) + expert_mix).astype(jnp.bfloat16)
    return (attn_branch, layer_out)


def solution(mesh):
    placed = (
        P("fsdp", None),
        P(),
        P(),
        P("fsdp", "grp"),
        P("fsdp", None),
        P("fsdp", None),
        P("grp", "fsdp"),
        P("fsdp", None),
        P("fsdp", None),
        P(("grp", "fsdp"), None, None),
        P(("grp", "fsdp"), None, None),
    )
    return jax.shard_map(
        on_device,
        mesh=mesh,
        in_specs=placed,
        out_specs=(P("fsdp", None), P("fsdp", "grp")),
        check_vma=False,
    )
```

```python
import functools

import jax
import jax.numpy as jnp
from jax import lax
from jax.experimental import pallas as pl
from jax.experimental.pallas import tpu as pltpu
from jax.sharding import PartitionSpec as P

KEY_VALUE_HEADS = 2
HEAD_DIMENSION = 128
FFW = 768


EPSILON = 1e-06
FLOOR_SCORE = -1e30
LOG2_E = 1.4426950408889634
SIDE = 4
PIECE_HEADS = 4
QUERY_TILE = 128
HIDDEN_TILE = 256
NORM_TILE = 64


def rms_scale(row_data, gain):
    floats = row_data.astype(jnp.float32)
    mean_sq = jnp.mean(floats * floats, axis=-1, keepdims=True)
    return (floats * lax.rsqrt(mean_sq + EPSILON) * gain).astype(jnp.bfloat16)


def to_other_core(rows):
    return lax.ppermute(rows, "fsdp", [(i, i ^ 1) for i in range(2 * SIDE * SIDE)])


def from_group(rows, shift):
    return lax.ppermute(rows, "grp", [((i + shift) % SIDE, i) for i in range(SIDE)])


def from_chips(rows):
    chips = SIDE * SIDE
    parts = lax.all_to_all(
        jnp.broadcast_to(rows[None], (chips, *rows.shape)),
        "fsdp",
        split_axis=0,
        concat_axis=0,
        axis_index_groups=[[2 * chip + core for chip in range(chips)] for core in range(2)],
        tiled=True,
    )
    return parts.reshape(chips * rows.shape[0], rows.shape[1])


def by_core(core, mine, other):
    return jnp.concatenate(
        [jnp.where(core == 0, mine, other), jnp.where(core == 0, other, mine)], axis=0
    )


def attend_kernel(
    rank_ref,
    query_ref,
    mine_ref,
    other_ref,
    out_ref,
    best,
    weighted,
    *,
    heads,
    first_head,
):
    rank = rank_ref[0]
    rows = query_ref.shape[0]
    span = 4 * rows
    core = rank % 2
    factor = HEAD_DIMENSION**-0.5 * LOG2_E
    best[...] = jnp.full_like(best, FLOOR_SCORE)
    weighted[...] = jnp.zeros_like(weighted)

    def step(index, masked):
        start = pl.multiple_of(index * span, span)
        mine = mine_ref[pl.ds(start, span), :]
        other = other_ref[pl.ds(start, span), :]
        keys = jnp.where(core == 0, mine, other)
        values = jnp.where(core == 0, other, mine)
        values = jnp.concatenate([values, jnp.ones_like(values)], axis=1)
        for head in range(heads):
            cols = slice((first_head + head) * HEAD_DIMENSION, (first_head + head + 1) * HEAD_DIMENSION)
            for row in range(0, rows, QUERY_TILE):
                tile = slice(row, row + QUERY_TILE)
                scores = lax.dot_general(
                    query_ref[tile, cols],
                    keys,
                    (((1,), (1,)), ((), ())),
                    preferred_element_type=jnp.float32,
                )
                if masked:
                    key_pos = lax.broadcasted_iota(jnp.int32, scores.shape, 1) + start
                    query_pos = lax.broadcasted_iota(jnp.int32, scores.shape, 0) + (
                        rank * rows + row
                    )
                    scores = jnp.where(key_pos <= query_pos, scores, FLOOR_SCORE)
                old = best[head, tile]
                new = jnp.maximum(old, jnp.max(scores, axis=1, keepdims=True))
                weights = jnp.exp2((scores - jnp.tile(new, (1, span // HEAD_DIMENSION))) * factor)
                rescale = jnp.exp2((old - new) * factor)
                best[head, tile] = new
                weighted[head, tile] = weighted[head, tile] * jnp.tile(rescale, (1, 2)) + jnp.dot(
                    weights.astype(jnp.bfloat16), values, preferred_element_type=jnp.float32
                )

    full = rank * rows // span

    def visit(index, carry):
        step(index, False)
        return carry

    lax.fori_loop(0, full, visit, 0)
    step(full, True)
    for head in range(heads):
        out_ref[:, head * HEAD_DIMENSION : (head + 1) * HEAD_DIMENSION] = (
            weighted[head, :, :HEAD_DIMENSION] / weighted[head, :, HEAD_DIMENSION:]
        ).astype(out_ref.dtype)


def attend(rank, query, gathered, first_head, heads):
    rows = query.shape[0]
    width = heads * HEAD_DIMENSION
    keys = gathered[0].shape[0]
    return pl.pallas_call(
        functools.partial(attend_kernel, heads=heads, first_head=first_head),
        out_shape=jax.ShapeDtypeStruct((rows, width), query.dtype),
        in_specs=[pl.BlockSpec(memory_space=pltpu.SMEM)]
        + [pl.BlockSpec(memory_space=pltpu.VMEM)] * (1 + len(gathered)),
        out_specs=pl.BlockSpec(memory_space=pltpu.VMEM),
        scratch_shapes=[
            pltpu.VMEM((heads, rows, HEAD_DIMENSION), jnp.float32),
            pltpu.VMEM((heads, rows, 2 * HEAD_DIMENSION), jnp.float32),
        ],
        compiler_params=pltpu.CompilerParams(vmem_limit_bytes=32 * 2**20),
        cost_estimate=pl.CostEstimate(
            flops=8 * rows * keys * width,
            bytes_accessed=4 * rows * width + 4 * keys * HEAD_DIMENSION,
            transcendentals=rows * keys * heads,
        ),
    )(rank, query, *gathered)


def project_kernel(group_ref, *refs, groups):
    part_refs, (weight_ref, *before, out_ref, total) = refs[:groups], refs[groups:]
    step = pl.program_id(0)
    weights = jnp.concatenate([weight_ref[0, i] for i in range(weight_ref.shape[1])], axis=1)

    for index in range(groups):

        @pl.when(step == index)
        def _(index=index):
            product = jnp.dot(part_refs[index][...], weights, preferred_element_type=jnp.float32)
            if index > 0:
                product += total[...]
            elif before:
                product += before[0][...]
            if index < groups - 1:
                total[...] = product
            else:
                out_ref[...] = product.astype(out_ref.dtype)


def project(group, parts, weights, piece, before, out_type):
    groups, blocks, _, block_cols = weights.shape
    rows, depth = parts[0].shape
    cols = blocks * block_cols
    whole = pl.BlockSpec((rows, cols), lambda i, group: (0, 0))
    return pl.pallas_call(
        functools.partial(project_kernel, groups=groups),
        grid_spec=pltpu.PrefetchScalarGridSpec(
            num_scalar_prefetch=1,
            grid=(groups,),
            in_specs=[pl.BlockSpec((rows, depth), lambda i, group: (0, 0))] * groups
            + [
                pl.BlockSpec(
                    (1, blocks, depth, block_cols),
                    lambda i, group: ((group[0] + i) % groups, 0, piece, 0),
                ),
            ]
            + [whole] * len(before),
            out_specs=whole,
            scratch_shapes=[pltpu.VMEM((rows, cols), jnp.float32)],
        ),
        out_shape=jax.ShapeDtypeStruct((rows, cols), out_type),
        compiler_params=pltpu.CompilerParams(vmem_limit_bytes=52 * 2**20),
        cost_estimate=pl.CostEstimate(
            flops=2 * groups * rows * depth * cols,
            bytes_accessed=2 * groups * depth * (rows + cols),
            transcendentals=0,
        ),
    )(group, *parts, weights, *before)


def expert_kernel(rows_ref, gain_ref, gate_ref, up_ref, down_ref, out_ref, normed, hidden, *, wide):
    step = pl.program_id(0)
    parts, rows, width = rows_ref.shape

    @pl.when(step == 0)
    def _():
        def scale_rows(index, carry):
            tile = pl.ds(pl.multiple_of(index * NORM_TILE, NORM_TILE), NORM_TILE)
            floats = [rows_ref[part, tile, :].astype(jnp.float32) for part in range(parts)]
            squares = sum(values * values for values in floats)
            mean_sq = jnp.sum(squares, axis=1, keepdims=True) / (parts * width)
            scale = lax.rsqrt(mean_sq + EPSILON)
            for part in range(parts):
                normed[part, tile, :] = (floats[part] * scale * gain_ref[part]).astype(jnp.bfloat16)
            return carry

        lax.fori_loop(0, rows // NORM_TILE, scale_rows, 0)

    @pl.when(step < wide)
    def _():
        def project(weight_ref):
            return sum(
                jnp.dot(
                    normed[part],
                    weight_ref[0, part * width : (part + 1) * width, :],
                    preferred_element_type=jnp.float32,
                )
                for part in range(parts)
            )

        hidden[step] = (jax.nn.silu(project(gate_ref)) * project(up_ref)).astype(jnp.bfloat16)

    @pl.when(step >= wide)
    def _():
        out_ref[0] = sum(
            jnp.dot(
                hidden[tile],
                down_ref[0, tile * HIDDEN_TILE : (tile + 1) * HIDDEN_TILE, :],
                preferred_element_type=jnp.float32,
            )
            for tile in range(wide)
        ).astype(out_ref.dtype)


def run_expert(arrived, gain, w_gate_up, w_down):
    parts, rows, width = arrived.shape
    model_width = parts * width
    wide = FFW // HIDDEN_TILE
    return pl.pallas_call(
        functools.partial(expert_kernel, wide=wide),
        grid=(wide + parts,),
        out_shape=jax.ShapeDtypeStruct(arrived.shape, arrived.dtype),
        in_specs=[
            pl.BlockSpec((parts, rows, width), lambda i: (0, 0, 0)),
            pl.BlockSpec((parts, 1, width), lambda i: (0, 0, 0)),
            pl.BlockSpec((1, model_width, HIDDEN_TILE), lambda i: (0, 0, jnp.minimum(i, wide - 1))),
            pl.BlockSpec(
                (1, model_width, HIDDEN_TILE), lambda i: (0, 0, wide + jnp.minimum(i, wide - 1))
            ),
            pl.BlockSpec((1, FFW, width), lambda i: (0, 0, jnp.maximum(i - wide, 0))),
        ],
        out_specs=pl.BlockSpec((1, rows, width), lambda i: (jnp.maximum(i - wide, 0), 0, 0)),
        scratch_shapes=[
            pltpu.VMEM((parts, rows, width), jnp.bfloat16),
            pltpu.VMEM((wide, rows, HIDDEN_TILE), jnp.bfloat16),
        ],
        compiler_params=pltpu.CompilerParams(vmem_limit_bytes=54 * 2**20),
        cost_estimate=pl.CostEstimate(
            flops=6 * rows * model_width * FFW,
            bytes_accessed=4 * rows * model_width + 6 * model_width * FFW,
            transcendentals=rows * FFW,
        ),
    )(arrived, gain.reshape(parts, 1, width), w_gate_up, w_gate_up, w_down)


def on_device(
    tokens,
    attn_gain,
    ffn_gain,
    w_query,
    w_key,
    value_weight,
    w_out,
    routes,
    route_probs,
    w_gate_up,
    w_down,
):
    head_groups = lax.axis_size("grp")
    fsdp_size = lax.axis_size("fsdp")
    current_group = lax.axis_index("grp")
    my_rank = lax.axis_index("fsdp")
    tok_rows, model_width = tokens.shape
    head_width = w_query.shape[1]
    col_width = model_width // head_groups
    key_value_head = current_group * KEY_VALUE_HEADS // head_groups
    key_cols = lax.dynamic_slice_in_dim(w_key, key_value_head * HEAD_DIMENSION, HEAD_DIMENSION, 1)
    value_cols = lax.dynamic_slice_in_dim(
        value_weight, key_value_head * HEAD_DIMENSION, HEAD_DIMENSION, 1
    )
    core = my_rank % 2
    w_query_all = lax.all_gather(w_query, "fsdp", axis=0, tiled=True)
    normed = lax.optimization_barrier(rms_scale(tokens, attn_gain))
    normed_other = to_other_core(normed)
    w_both, normed = lax.optimization_barrier((jnp.stack([key_cols, value_cols]), normed))
    w_kv = lax.all_to_all(
        jnp.tile(w_both, (fsdp_size // 2, 1, 1)), "fsdp", split_axis=0, concat_axis=0, tiled=True
    ).reshape(model_width, HEAD_DIMENSION)

    def project_kv(rows):
        return jnp.dot(rows, w_kv, preferred_element_type=jnp.float32).astype(jnp.bfloat16)

    kv_local = by_core(core, project_kv(normed), project_kv(normed_other))
    w_out_block, w_kv = lax.optimization_barrier((w_out, w_kv))
    w_turned = lax.ppermute(
        w_out_block,
        ("grp", "fsdp"),
        [
            (g * fsdp_size + f, f // 8 * fsdp_size + g * 8 + f % 8)
            for g in range(head_groups)
            for f in range(fsdp_size)
        ],
    )
    w_turned, kv_local = lax.optimization_barrier((w_turned, kv_local))
    w_out_all = lax.all_gather(w_turned, "fsdp", axis=0, tiled=True)
    kv_mine = from_chips(kv_local)
    query = jnp.dot(normed, w_query_all, preferred_element_type=jnp.float32).astype(jnp.bfloat16)
    kv_mine, query = lax.optimization_barrier((kv_mine, query))
    gathered = (kv_mine, to_other_core(kv_mine))
    rank_array = my_rank.astype(jnp.int32).reshape(1)
    pieces = []
    for head in range(0, head_width // HEAD_DIMENSION, PIECE_HEADS):
        piece = attend(rank_array, query, gathered, head, PIECE_HEADS)
        pieces.append([piece] + [from_group(piece, shift) for shift in range(1, head_groups)])
    w_out_cols = w_out_all.reshape(head_groups, fsdp_size // head_groups, *w_out.shape)
    group_array = current_group.astype(jnp.int32).reshape(1)
    before = []
    for index, piece in enumerate(pieces):
        out_type = jnp.bfloat16 if index == len(pieces) - 1 else jnp.float32
        before = [project(group_array, piece, w_out_cols, index, before, out_type)]
    (branch_cols,) = before
    own_cols = lax.dynamic_slice_in_dim(tokens, current_group * col_width, col_width, 1)
    resid = (own_cols.astype(jnp.float32) + branch_cols.astype(jnp.float32)).astype(jnp.bfloat16)

    top_count = routes.shape[1]
    experts_all = head_groups * fsdp_size
    capacity = max(2, 3 * tok_rows * top_count // (2 * experts_all))
    slots = experts_all * capacity
    expert_ids = jnp.arange(experts_all, dtype=jnp.int32)
    named = routes[:, :, None] == expert_ids[None, None, :]
    hits = jnp.any(named, axis=1)
    token_ids = jnp.arange(tok_rows, dtype=jnp.int32)
    earlier = (token_ids[None, :] < token_ids[:, None]).astype(jnp.bfloat16)
    rank = jnp.dot(earlier, hits.astype(jnp.bfloat16), preferred_element_type=jnp.float32)
    code = jnp.where(hits, rank, -1.0).astype(jnp.bfloat16)
    slot_list = jnp.arange(slots, dtype=jnp.int32)
    spread = (slot_list[None, :] // capacity == expert_ids[:, None]).astype(jnp.bfloat16)
    code_slots = jnp.dot(code, spread, preferred_element_type=jnp.float32)
    slot_match = code_slots == (slot_list % capacity).astype(jnp.float32)[None, :]
    chosen = slot_match.astype(jnp.bfloat16)
    named_probs = jnp.sum(jnp.where(named, route_probs[:, :, None], 0.0), axis=1)
    prob_slots = jnp.dot(
        named_probs.astype(jnp.bfloat16), spread, preferred_element_type=jnp.float32
    )
    mixing = lax.optimization_barrier(jnp.where(slot_match, prob_slots, 0.0).astype(jnp.bfloat16))

    outbound = lax.dot_general(
        chosen, resid, (((0,), (0,)), ((), ())), preferred_element_type=jnp.float32
    ).astype(jnp.bfloat16)
    arrived = lax.all_to_all(
        outbound.reshape(experts_all, capacity, col_width),
        ("grp", "fsdp"),
        split_axis=0,
        concat_axis=0,
        tiled=True,
    )
    arrived, branch_cols = lax.optimization_barrier((arrived, branch_cols))
    blocks = [branch_cols] + [from_group(branch_cols, shift) for shift in range(1, head_groups)]
    result = run_expert(
        arrived.reshape(head_groups, fsdp_size * capacity, col_width), ffn_gain, w_gate_up, w_down
    )
    result, blocks = lax.optimization_barrier((result, blocks))
    attn_branch = jnp.concatenate(
        [
            lax.select_n(lax.rem(group + head_groups - current_group, head_groups), *blocks)
            for group in range(head_groups)
        ],
        axis=1,
    )
    returned = lax.all_to_all(
        result.reshape(experts_all, capacity, col_width),
        ("grp", "fsdp"),
        split_axis=0,
        concat_axis=0,
        tiled=True,
    )
    expert_mix = jnp.dot(
        mixing, returned.reshape(slots, col_width), preferred_element_type=jnp.float32
    )
    layer_out = (resid.astype(jnp.float32) + expert_mix).astype(jnp.bfloat16)
    return (attn_branch, layer_out)


def solution(mesh):
    placed = (
        P("fsdp", None),
        P(),
        P(),
        P("fsdp", "grp"),
        P("fsdp", None),
        P("fsdp", None),
        P("grp", "fsdp"),
        P("fsdp", None),
        P("fsdp", None),
        P(("grp", "fsdp"), None, None),
        P(("grp", "fsdp"), None, None),
    )
    return jax.shard_map(
        on_device,
        mesh=mesh,
        in_specs=placed,
        out_specs=(P("fsdp", None), P("fsdp", "grp")),
        check_vma=False,
    )
```

```python
import functools

import jax
import jax.numpy as jnp
from jax import lax
from jax.experimental import pallas as pl
from jax.experimental.pallas import tpu as pltpu
from jax.sharding import PartitionSpec as P

KEY_VALUE_HEADS = 2
HEAD_DIMENSION = 128
FFW = 768


EPSILON = 1e-06
FLOOR_SCORE = -1e30
LOG2_E = 1.4426950408889634
SIDE = 4
PIECE_HEADS = 4
QUERY_TILE = 128
HIDDEN_TILE = 256
NORM_TILE = 64
EXPERT_VMEM = 40


def rms_scale(row_data, gain):
    floats = row_data.astype(jnp.float32)
    mean_sq = jnp.mean(floats * floats, axis=-1, keepdims=True)
    return (floats * lax.rsqrt(mean_sq + EPSILON) * gain).astype(jnp.bfloat16)


def to_other_core(rows):
    return lax.ppermute(rows, "fsdp", [(i, i ^ 1) for i in range(2 * SIDE * SIDE)])


def from_group(rows, shift):
    return lax.ppermute(rows, "grp", [((i + shift) % SIDE, i) for i in range(SIDE)])


def from_chips(rows):
    chips = SIDE * SIDE
    parts = lax.all_to_all(
        jnp.broadcast_to(rows[None], (chips, *rows.shape)),
        "fsdp",
        split_axis=0,
        concat_axis=0,
        axis_index_groups=[[2 * chip + core for chip in range(chips)] for core in range(2)],
        tiled=True,
    )
    return parts.reshape(chips * rows.shape[0], rows.shape[1])


def by_core(core, mine, other):
    return jnp.concatenate(
        [jnp.where(core == 0, mine, other), jnp.where(core == 0, other, mine)], axis=0
    )


def attend_kernel(
    rank_ref,
    query_ref,
    mine_ref,
    other_ref,
    out_ref,
    best,
    weighted,
    *,
    heads,
    first_head,
):
    rank = rank_ref[0]
    rows = query_ref.shape[0]
    span = 4 * rows
    core = rank % 2
    factor = HEAD_DIMENSION**-0.5 * LOG2_E
    best[...] = jnp.full_like(best, FLOOR_SCORE)
    weighted[...] = jnp.zeros_like(weighted)

    def step(index, masked):
        start = pl.multiple_of(index * span, span)
        mine = mine_ref[pl.ds(start, span), :]
        other = other_ref[pl.ds(start, span), :]
        keys = jnp.where(core == 0, mine, other)
        values = jnp.where(core == 0, other, mine)
        values = jnp.concatenate([values, jnp.ones_like(values)], axis=1)
        for head in range(heads):
            cols = slice((first_head + head) * HEAD_DIMENSION, (first_head + head + 1) * HEAD_DIMENSION)
            for row in range(0, rows, QUERY_TILE):
                tile = slice(row, row + QUERY_TILE)
                scores = lax.dot_general(
                    query_ref[tile, cols],
                    keys,
                    (((1,), (1,)), ((), ())),
                    preferred_element_type=jnp.float32,
                )
                if masked:
                    key_pos = lax.broadcasted_iota(jnp.int32, scores.shape, 1) + start
                    query_pos = lax.broadcasted_iota(jnp.int32, scores.shape, 0) + (
                        rank * rows + row
                    )
                    scores = jnp.where(key_pos <= query_pos, scores, FLOOR_SCORE)
                old = best[head, tile]
                new = jnp.maximum(old, jnp.max(scores, axis=1, keepdims=True))
                weights = jnp.exp2((scores - jnp.tile(new, (1, span // HEAD_DIMENSION))) * factor)
                rescale = jnp.exp2((old - new) * factor)
                best[head, tile] = new
                weighted[head, tile] = weighted[head, tile] * jnp.tile(rescale, (1, 2)) + jnp.dot(
                    weights.astype(jnp.bfloat16), values, preferred_element_type=jnp.float32
                )

    full = rank * rows // span

    def visit(index, carry):
        step(index, False)
        return carry

    lax.fori_loop(0, full, visit, 0)
    step(full, True)
    for head in range(heads):
        out_ref[:, head * HEAD_DIMENSION : (head + 1) * HEAD_DIMENSION] = (
            weighted[head, :, :HEAD_DIMENSION] / weighted[head, :, HEAD_DIMENSION:]
        ).astype(out_ref.dtype)


def attend(rank, query, gathered, first_head, heads):
    rows = query.shape[0]
    width = heads * HEAD_DIMENSION
    keys = gathered[0].shape[0]
    return pl.pallas_call(
        functools.partial(attend_kernel, heads=heads, first_head=first_head),
        out_shape=jax.ShapeDtypeStruct((rows, width), query.dtype),
        in_specs=[pl.BlockSpec(memory_space=pltpu.SMEM)]
        + [pl.BlockSpec(memory_space=pltpu.VMEM)] * (1 + len(gathered)),
        out_specs=pl.BlockSpec(memory_space=pltpu.VMEM),
        scratch_shapes=[
            pltpu.VMEM((heads, rows, HEAD_DIMENSION), jnp.float32),
            pltpu.VMEM((heads, rows, 2 * HEAD_DIMENSION), jnp.float32),
        ],
        compiler_params=pltpu.CompilerParams(vmem_limit_bytes=32 * 2**20),
        cost_estimate=pl.CostEstimate(
            flops=8 * rows * keys * width,
            bytes_accessed=4 * rows * width + 4 * keys * HEAD_DIMENSION,
            transcendentals=rows * keys * heads,
        ),
    )(rank, query, *gathered)


def project_kernel(group_ref, *refs, groups):
    part_refs, (weight_ref, *before, out_ref, total) = refs[:groups], refs[groups:]
    step = pl.program_id(0)
    weights = jnp.concatenate([weight_ref[0, i] for i in range(weight_ref.shape[1])], axis=1)

    for index in range(groups):

        @pl.when(step == index)
        def _(index=index):
            product = jnp.dot(part_refs[index][...], weights, preferred_element_type=jnp.float32)
            if index > 0:
                product += total[...]
            elif before:
                product += before[0][...]
            if index < groups - 1:
                total[...] = product
            else:
                out_ref[...] = product.astype(out_ref.dtype)


def project(group, parts, weights, piece, before, out_type):
    groups, blocks, _, block_cols = weights.shape
    rows, depth = parts[0].shape
    cols = blocks * block_cols
    whole = pl.BlockSpec((rows, cols), lambda i, group: (0, 0))
    return pl.pallas_call(
        functools.partial(project_kernel, groups=groups),
        grid_spec=pltpu.PrefetchScalarGridSpec(
            num_scalar_prefetch=1,
            grid=(groups,),
            in_specs=[pl.BlockSpec((rows, depth), lambda i, group: (0, 0))] * groups
            + [
                pl.BlockSpec(
                    (1, blocks, depth, block_cols),
                    lambda i, group: ((group[0] + i) % groups, 0, piece, 0),
                ),
            ]
            + [whole] * len(before),
            out_specs=whole,
            scratch_shapes=[pltpu.VMEM((rows, cols), jnp.float32)],
        ),
        out_shape=jax.ShapeDtypeStruct((rows, cols), out_type),
        compiler_params=pltpu.CompilerParams(vmem_limit_bytes=52 * 2**20),
        cost_estimate=pl.CostEstimate(
            flops=2 * groups * rows * depth * cols,
            bytes_accessed=2 * groups * depth * (rows + cols),
            transcendentals=0,
        ),
    )(group, *parts, weights, *before)


def expert_kernel(rows_ref, gain_ref, gate_ref, up_ref, down_ref, out_ref, normed, hidden, *, wide):
    step = pl.program_id(0)
    parts, rows, width = rows_ref.shape

    @pl.when(step == 0)
    def _():
        def scale_rows(index, carry):
            tile = pl.ds(pl.multiple_of(index * NORM_TILE, NORM_TILE), NORM_TILE)
            floats = [rows_ref[part, tile, :].astype(jnp.float32) for part in range(parts)]
            squares = sum(values * values for values in floats)
            mean_sq = jnp.sum(squares, axis=1, keepdims=True) / (parts * width)
            scale = lax.rsqrt(mean_sq + EPSILON)
            for part in range(parts):
                normed[part, tile, :] = (floats[part] * scale * gain_ref[part]).astype(jnp.bfloat16)
            return carry

        lax.fori_loop(0, rows // NORM_TILE, scale_rows, 0)

    @pl.when(step < wide)
    def _():
        def project(weight_ref):
            return sum(
                jnp.dot(
                    normed[part],
                    weight_ref[0, part * width : (part + 1) * width, :],
                    preferred_element_type=jnp.float32,
                )
                for part in range(parts)
            )

        hidden[step] = (jax.nn.silu(project(gate_ref)) * project(up_ref)).astype(jnp.bfloat16)

    @pl.when(step >= wide)
    def _():
        out_ref[0] = sum(
            jnp.dot(
                hidden[tile],
                down_ref[0, tile * HIDDEN_TILE : (tile + 1) * HIDDEN_TILE, :],
                preferred_element_type=jnp.float32,
            )
            for tile in range(wide)
        ).astype(out_ref.dtype)


def run_expert(arrived, gain, w_gate_up, w_down):
    parts, rows, width = arrived.shape
    model_width = parts * width
    wide = FFW // HIDDEN_TILE
    return pl.pallas_call(
        functools.partial(expert_kernel, wide=wide),
        grid=(wide + parts,),
        out_shape=jax.ShapeDtypeStruct(arrived.shape, arrived.dtype),
        in_specs=[
            pl.BlockSpec(memory_space=pltpu.VMEM),
            pl.BlockSpec(memory_space=pltpu.VMEM),
            pl.BlockSpec((1, model_width, HIDDEN_TILE), lambda i: (0, 0, jnp.minimum(i, wide - 1))),
            pl.BlockSpec(
                (1, model_width, HIDDEN_TILE), lambda i: (0, 0, wide + jnp.minimum(i, wide - 1))
            ),
            pl.BlockSpec((1, FFW, width), lambda i: (0, 0, jnp.maximum(i - wide, 0))),
        ],
        out_specs=pl.BlockSpec((1, rows, width), lambda i: (jnp.maximum(i - wide, 0), 0, 0)),
        scratch_shapes=[
            pltpu.VMEM((parts, rows, width), jnp.bfloat16),
            pltpu.VMEM((wide, rows, HIDDEN_TILE), jnp.bfloat16),
        ],
        compiler_params=pltpu.CompilerParams(vmem_limit_bytes=EXPERT_VMEM * 2**20),
        cost_estimate=pl.CostEstimate(
            flops=6 * rows * model_width * FFW,
            bytes_accessed=4 * rows * model_width + 6 * model_width * FFW,
            transcendentals=rows * FFW,
        ),
    )(arrived, gain.reshape(parts, 1, width), w_gate_up, w_gate_up, w_down)


def on_device(
    tokens,
    attn_gain,
    ffn_gain,
    w_query,
    w_key,
    value_weight,
    w_out,
    routes,
    route_probs,
    w_gate_up,
    w_down,
):
    head_groups = lax.axis_size("grp")
    fsdp_size = lax.axis_size("fsdp")
    current_group = lax.axis_index("grp")
    my_rank = lax.axis_index("fsdp")
    tok_rows, model_width = tokens.shape
    head_width = w_query.shape[1]
    col_width = model_width // head_groups
    key_value_head = current_group * KEY_VALUE_HEADS // head_groups
    key_cols = lax.dynamic_slice_in_dim(w_key, key_value_head * HEAD_DIMENSION, HEAD_DIMENSION, 1)
    value_cols = lax.dynamic_slice_in_dim(
        value_weight, key_value_head * HEAD_DIMENSION, HEAD_DIMENSION, 1
    )
    core = my_rank % 2
    w_query_all = lax.all_gather(w_query, "fsdp", axis=0, tiled=True)
    normed = lax.optimization_barrier(rms_scale(tokens, attn_gain))
    normed_other = to_other_core(normed)
    w_both, normed = lax.optimization_barrier((jnp.stack([key_cols, value_cols]), normed))
    w_kv = lax.all_to_all(
        jnp.tile(w_both, (fsdp_size // 2, 1, 1)), "fsdp", split_axis=0, concat_axis=0, tiled=True
    ).reshape(model_width, HEAD_DIMENSION)

    def project_kv(rows):
        return jnp.dot(rows, w_kv, preferred_element_type=jnp.float32).astype(jnp.bfloat16)

    kv_local = by_core(core, project_kv(normed), project_kv(normed_other))
    w_out_block, w_kv = lax.optimization_barrier((w_out, w_kv))
    w_turned = lax.ppermute(
        w_out_block,
        ("grp", "fsdp"),
        [
            (g * fsdp_size + f, f // 8 * fsdp_size + g * 8 + f % 8)
            for g in range(head_groups)
            for f in range(fsdp_size)
        ],
    )
    w_turned, kv_local = lax.optimization_barrier((w_turned, kv_local))
    w_out_all = lax.all_gather(w_turned, "fsdp", axis=0, tiled=True)
    kv_mine = from_chips(kv_local)
    query = jnp.dot(normed, w_query_all, preferred_element_type=jnp.float32).astype(jnp.bfloat16)
    kv_mine, query = lax.optimization_barrier((kv_mine, query))
    gathered = (kv_mine, to_other_core(kv_mine))
    rank_array = my_rank.astype(jnp.int32).reshape(1)
    pieces = []
    for head in range(0, head_width // HEAD_DIMENSION, PIECE_HEADS):
        piece = attend(rank_array, query, gathered, head, PIECE_HEADS)
        pieces.append([piece] + [from_group(piece, shift) for shift in range(1, head_groups)])
    w_out_cols = w_out_all.reshape(head_groups, fsdp_size // head_groups, *w_out.shape)
    group_array = current_group.astype(jnp.int32).reshape(1)
    before = []
    for index, piece in enumerate(pieces):
        out_type = jnp.bfloat16 if index == len(pieces) - 1 else jnp.float32
        before = [project(group_array, piece, w_out_cols, index, before, out_type)]
    (branch_cols,) = before
    own_cols = lax.dynamic_slice_in_dim(tokens, current_group * col_width, col_width, 1)
    resid = (own_cols.astype(jnp.float32) + branch_cols.astype(jnp.float32)).astype(jnp.bfloat16)

    top_count = routes.shape[1]
    experts_all = head_groups * fsdp_size
    capacity = max(2, 3 * tok_rows * top_count // (2 * experts_all))
    slots = experts_all * capacity
    expert_ids = jnp.arange(experts_all, dtype=jnp.int32)
    named = routes[:, :, None] == expert_ids[None, None, :]
    hits = jnp.any(named, axis=1)
    token_ids = jnp.arange(tok_rows, dtype=jnp.int32)
    earlier = (token_ids[None, :] < token_ids[:, None]).astype(jnp.bfloat16)
    rank = jnp.dot(earlier, hits.astype(jnp.bfloat16), preferred_element_type=jnp.float32)
    code = jnp.where(hits, rank, -1.0).astype(jnp.bfloat16)
    slot_list = jnp.arange(slots, dtype=jnp.int32)
    spread = (slot_list[None, :] // capacity == expert_ids[:, None]).astype(jnp.bfloat16)
    code_slots = jnp.dot(code, spread, preferred_element_type=jnp.float32)
    slot_match = code_slots == (slot_list % capacity).astype(jnp.float32)[None, :]
    chosen = slot_match.astype(jnp.bfloat16)
    named_probs = jnp.sum(jnp.where(named, route_probs[:, :, None], 0.0), axis=1)
    prob_slots = jnp.dot(
        named_probs.astype(jnp.bfloat16), spread, preferred_element_type=jnp.float32
    )
    mixing = lax.optimization_barrier(jnp.where(slot_match, prob_slots, 0.0).astype(jnp.bfloat16))

    outbound = lax.dot_general(
        chosen, resid, (((0,), (0,)), ((), ())), preferred_element_type=jnp.float32
    ).astype(jnp.bfloat16)
    arrived = lax.all_to_all(
        outbound.reshape(experts_all, capacity, col_width),
        ("grp", "fsdp"),
        split_axis=0,
        concat_axis=0,
        tiled=True,
    )
    arrived, branch_cols = lax.optimization_barrier((arrived, branch_cols))
    blocks = [branch_cols] + [from_group(branch_cols, shift) for shift in range(1, head_groups)]
    result = run_expert(
        arrived.reshape(head_groups, fsdp_size * capacity, col_width), ffn_gain, w_gate_up, w_down
    )
    result, blocks = lax.optimization_barrier((result, blocks))
    attn_branch = jnp.concatenate(
        [
            lax.select_n(lax.rem(group + head_groups - current_group, head_groups), *blocks)
            for group in range(head_groups)
        ],
        axis=1,
    )
    returned = lax.all_to_all(
        result.reshape(experts_all, capacity, col_width),
        ("grp", "fsdp"),
        split_axis=0,
        concat_axis=0,
        tiled=True,
    )
    expert_mix = jnp.dot(
        mixing, returned.reshape(slots, col_width), preferred_element_type=jnp.float32
    )
    layer_out = (resid.astype(jnp.float32) + expert_mix).astype(jnp.bfloat16)
    return (attn_branch, layer_out)


def solution(mesh):
    placed = (
        P("fsdp", None),
        P(),
        P(),
        P("fsdp", "grp"),
        P("fsdp", None),
        P("fsdp", None),
        P("grp", "fsdp"),
        P("fsdp", None),
        P("fsdp", None),
        P(("grp", "fsdp"), None, None),
        P(("grp", "fsdp"), None, None),
    )
    return jax.shard_map(
        on_device,
        mesh=mesh,
        in_specs=placed,
        out_specs=(P("fsdp", None), P("fsdp", "grp")),
        check_vma=False,
    )
```

```python
import functools

import jax
import jax.numpy as jnp
from jax import lax
from jax.experimental import pallas as pl
from jax.experimental.pallas import tpu as pltpu
from jax.sharding import PartitionSpec as P

KEY_VALUE_HEADS = 2
HEAD_DIMENSION = 128
FFW = 768


EPSILON = 1e-06
FLOOR_SCORE = -1e30
LOG2_E = 1.4426950408889634
SIDE = 4
PIECE_HEADS = 4
QUERY_TILE = 128
HIDDEN_TILE = 256
NORM_TILE = 64
EXPERT_VMEM = 40


def rms_scale(row_data, gain):
    floats = row_data.astype(jnp.float32)
    mean_sq = jnp.mean(floats * floats, axis=-1, keepdims=True)
    return (floats * lax.rsqrt(mean_sq + EPSILON) * gain).astype(jnp.bfloat16)


def to_other_core(rows):
    return lax.ppermute(rows, "fsdp", [(i, i ^ 1) for i in range(2 * SIDE * SIDE)])


def from_group(rows, shift):
    return lax.ppermute(rows, "grp", [((i + shift) % SIDE, i) for i in range(SIDE)])


def from_chips(rows):
    chips = SIDE * SIDE
    parts = lax.all_to_all(
        jnp.broadcast_to(rows[None], (chips, *rows.shape)),
        "fsdp",
        split_axis=0,
        concat_axis=0,
        axis_index_groups=[[2 * chip + core for chip in range(chips)] for core in range(2)],
        tiled=True,
    )
    return parts.reshape(chips * rows.shape[0], rows.shape[1])


def by_core(core, mine, other):
    return jnp.concatenate(
        [jnp.where(core == 0, mine, other), jnp.where(core == 0, other, mine)], axis=0
    )


def attend_kernel(
    rank_ref,
    query_ref,
    mine_ref,
    other_ref,
    out_ref,
    best,
    weighted,
    *,
    heads,
    first_head,
):
    rank = rank_ref[0]
    rows = query_ref.shape[0]
    span = 4 * rows
    core = rank % 2
    factor = HEAD_DIMENSION**-0.5 * LOG2_E
    best[...] = jnp.full_like(best, FLOOR_SCORE)
    weighted[...] = jnp.zeros_like(weighted)

    def step(index, masked):
        start = pl.multiple_of(index * span, span)
        mine = mine_ref[pl.ds(start, span), :]
        other = other_ref[pl.ds(start, span), :]
        keys = jnp.where(core == 0, mine, other)
        values = jnp.where(core == 0, other, mine)
        values = jnp.concatenate([values, jnp.ones_like(values)], axis=1)
        for head in range(heads):
            cols = slice((first_head + head) * HEAD_DIMENSION, (first_head + head + 1) * HEAD_DIMENSION)
            for row in range(0, rows, QUERY_TILE):
                tile = slice(row, row + QUERY_TILE)
                scores = lax.dot_general(
                    query_ref[tile, cols],
                    keys,
                    (((1,), (1,)), ((), ())),
                    preferred_element_type=jnp.float32,
                )
                if masked:
                    key_pos = lax.broadcasted_iota(jnp.int32, scores.shape, 1) + start
                    query_pos = lax.broadcasted_iota(jnp.int32, scores.shape, 0) + (
                        rank * rows + row
                    )
                    scores = jnp.where(key_pos <= query_pos, scores, FLOOR_SCORE)
                old = best[head, tile]
                new = jnp.maximum(old, jnp.max(scores, axis=1, keepdims=True))
                weights = jnp.exp2((scores - jnp.tile(new, (1, span // HEAD_DIMENSION))) * factor)
                rescale = jnp.exp2((old - new) * factor)
                best[head, tile] = new
                weighted[head, tile] = weighted[head, tile] * jnp.tile(rescale, (1, 2)) + jnp.dot(
                    weights.astype(jnp.bfloat16), values, preferred_element_type=jnp.float32
                )

    full = rank * rows // span

    def visit(index, carry):
        step(index, False)
        return carry

    lax.fori_loop(0, full, visit, 0)
    step(full, True)
    for head in range(heads):
        out_ref[:, head * HEAD_DIMENSION : (head + 1) * HEAD_DIMENSION] = (
            weighted[head, :, :HEAD_DIMENSION] / weighted[head, :, HEAD_DIMENSION:]
        ).astype(out_ref.dtype)


def attend(rank, query, gathered, first_head, heads):
    rows = query.shape[0]
    width = heads * HEAD_DIMENSION
    keys = gathered[0].shape[0]
    return pl.pallas_call(
        functools.partial(attend_kernel, heads=heads, first_head=first_head),
        out_shape=jax.ShapeDtypeStruct((rows, width), query.dtype),
        in_specs=[pl.BlockSpec(memory_space=pltpu.SMEM)]
        + [pl.BlockSpec(memory_space=pltpu.VMEM)] * (1 + len(gathered)),
        out_specs=pl.BlockSpec(memory_space=pltpu.VMEM),
        scratch_shapes=[
            pltpu.VMEM((heads, rows, HEAD_DIMENSION), jnp.float32),
            pltpu.VMEM((heads, rows, 2 * HEAD_DIMENSION), jnp.float32),
        ],
        compiler_params=pltpu.CompilerParams(vmem_limit_bytes=32 * 2**20),
        cost_estimate=pl.CostEstimate(
            flops=8 * rows * keys * width,
            bytes_accessed=4 * rows * width + 4 * keys * HEAD_DIMENSION,
            transcendentals=rows * keys * heads,
        ),
    )(rank, query, *gathered)


def project_kernel(group_ref, *refs, groups):
    part_refs, (weight_ref, *before, out_ref, total) = refs[:groups], refs[groups:]
    step = pl.program_id(0)
    weights = jnp.concatenate([weight_ref[0, i] for i in range(weight_ref.shape[1])], axis=1)

    for index in range(groups):

        @pl.when(step == index)
        def _(index=index):
            product = jnp.dot(part_refs[index][...], weights, preferred_element_type=jnp.float32)
            if index > 0:
                product += total[...]
            elif before:
                product += before[0][...]
            if index < groups - 1:
                total[...] = product
            else:
                out_ref[...] = product.astype(out_ref.dtype)


def project(group, parts, weights, piece, before, out_type):
    groups, blocks, _, block_cols = weights.shape
    rows, depth = parts[0].shape
    cols = blocks * block_cols
    whole = pl.BlockSpec((rows, cols), lambda i, group: (0, 0))
    return pl.pallas_call(
        functools.partial(project_kernel, groups=groups),
        grid_spec=pltpu.PrefetchScalarGridSpec(
            num_scalar_prefetch=1,
            grid=(groups,),
            in_specs=[pl.BlockSpec((rows, depth), lambda i, group: (0, 0))] * groups
            + [
                pl.BlockSpec(
                    (1, blocks, depth, block_cols),
                    lambda i, group: ((group[0] + i) % groups, 0, piece, 0),
                ),
            ]
            + [whole] * len(before),
            out_specs=whole,
            scratch_shapes=[pltpu.VMEM((rows, cols), jnp.float32)],
        ),
        out_shape=jax.ShapeDtypeStruct((rows, cols), out_type),
        compiler_params=pltpu.CompilerParams(vmem_limit_bytes=52 * 2**20),
        cost_estimate=pl.CostEstimate(
            flops=2 * groups * rows * depth * cols,
            bytes_accessed=2 * groups * depth * (rows + cols),
            transcendentals=0,
        ),
    )(group, *parts, weights, *before)


def expert_kernel(rows_ref, gain_ref, gate_ref, up_ref, down_ref, out_ref, normed, hidden, *, wide):
    step = pl.program_id(0)
    parts, rows, width = rows_ref.shape

    @pl.when(step == 0)
    def _():
        def scale_rows(index, carry):
            tile = pl.ds(pl.multiple_of(index * NORM_TILE, NORM_TILE), NORM_TILE)
            floats = [rows_ref[part, tile, :].astype(jnp.float32) for part in range(parts)]
            squares = sum(values * values for values in floats)
            mean_sq = jnp.sum(squares, axis=1, keepdims=True) / (parts * width)
            scale = lax.rsqrt(mean_sq + EPSILON)
            for part in range(parts):
                normed[part, tile, :] = (floats[part] * scale * gain_ref[part]).astype(jnp.bfloat16)
            return carry

        lax.fori_loop(0, rows // NORM_TILE, scale_rows, 0)

    @pl.when(step < wide)
    def _():
        def project(weight_ref):
            return sum(
                jnp.dot(
                    normed[part],
                    weight_ref[0, part * width : (part + 1) * width, :],
                    preferred_element_type=jnp.float32,
                )
                for part in range(parts)
            )

        hidden[step] = (jax.nn.silu(project(gate_ref)) * project(up_ref)).astype(jnp.bfloat16)

    @pl.when(step >= wide)
    def _():
        out_ref[0] = sum(
            jnp.dot(
                hidden[tile],
                down_ref[0, tile * HIDDEN_TILE : (tile + 1) * HIDDEN_TILE, :],
                preferred_element_type=jnp.float32,
            )
            for tile in range(wide)
        ).astype(out_ref.dtype)


def run_expert(arrived, gain, w_gate_up, w_down):
    parts, rows, width = arrived.shape
    model_width = parts * width
    wide = FFW // HIDDEN_TILE
    return pl.pallas_call(
        functools.partial(expert_kernel, wide=wide),
        grid=(wide + parts,),
        out_shape=pltpu.HBM(arrived.shape, arrived.dtype),
        in_specs=[
            pl.BlockSpec(memory_space=pltpu.VMEM),
            pl.BlockSpec(memory_space=pltpu.VMEM),
            pl.BlockSpec((1, model_width, HIDDEN_TILE), lambda i: (0, 0, jnp.minimum(i, wide - 1))),
            pl.BlockSpec(
                (1, model_width, HIDDEN_TILE), lambda i: (0, 0, wide + jnp.minimum(i, wide - 1))
            ),
            pl.BlockSpec((1, FFW, width), lambda i: (0, 0, jnp.maximum(i - wide, 0))),
        ],
        out_specs=pl.BlockSpec((1, rows, width), lambda i: (jnp.maximum(i - wide, 0), 0, 0)),
        scratch_shapes=[
            pltpu.VMEM((parts, rows, width), jnp.bfloat16),
            pltpu.VMEM((wide, rows, HIDDEN_TILE), jnp.bfloat16),
        ],
        compiler_params=pltpu.CompilerParams(vmem_limit_bytes=EXPERT_VMEM * 2**20),
        cost_estimate=pl.CostEstimate(
            flops=6 * rows * model_width * FFW,
            bytes_accessed=4 * rows * model_width + 6 * model_width * FFW,
            transcendentals=rows * FFW,
        ),
    )(arrived, gain.reshape(parts, 1, width), w_gate_up, w_gate_up, w_down)


def on_device(
    tokens,
    attn_gain,
    ffn_gain,
    w_query,
    w_key,
    value_weight,
    w_out,
    routes,
    route_probs,
    w_gate_up,
    w_down,
):
    head_groups = lax.axis_size("grp")
    fsdp_size = lax.axis_size("fsdp")
    current_group = lax.axis_index("grp")
    my_rank = lax.axis_index("fsdp")
    tok_rows, model_width = tokens.shape
    head_width = w_query.shape[1]
    col_width = model_width // head_groups
    key_value_head = current_group * KEY_VALUE_HEADS // head_groups
    key_cols = lax.dynamic_slice_in_dim(w_key, key_value_head * HEAD_DIMENSION, HEAD_DIMENSION, 1)
    value_cols = lax.dynamic_slice_in_dim(
        value_weight, key_value_head * HEAD_DIMENSION, HEAD_DIMENSION, 1
    )
    core = my_rank % 2
    w_query_all = lax.all_gather(w_query, "fsdp", axis=0, tiled=True)
    normed = lax.optimization_barrier(rms_scale(tokens, attn_gain))
    normed_other = to_other_core(normed)
    w_both, normed = lax.optimization_barrier((jnp.stack([key_cols, value_cols]), normed))
    w_kv = lax.all_to_all(
        jnp.tile(w_both, (fsdp_size // 2, 1, 1)), "fsdp", split_axis=0, concat_axis=0, tiled=True
    ).reshape(model_width, HEAD_DIMENSION)

    def project_kv(rows):
        return jnp.dot(rows, w_kv, preferred_element_type=jnp.float32).astype(jnp.bfloat16)

    kv_local = by_core(core, project_kv(normed), project_kv(normed_other))
    w_out_block, w_kv = lax.optimization_barrier((w_out, w_kv))
    w_turned = lax.ppermute(
        w_out_block,
        ("grp", "fsdp"),
        [
            (g * fsdp_size + f, f // 8 * fsdp_size + g * 8 + f % 8)
            for g in range(head_groups)
            for f in range(fsdp_size)
        ],
    )
    w_turned, kv_local = lax.optimization_barrier((w_turned, kv_local))
    w_out_all = lax.all_gather(w_turned, "fsdp", axis=0, tiled=True)
    kv_mine = from_chips(kv_local)
    query = jnp.dot(normed, w_query_all, preferred_element_type=jnp.float32).astype(jnp.bfloat16)
    kv_mine, query = lax.optimization_barrier((kv_mine, query))
    gathered = (kv_mine, to_other_core(kv_mine))
    rank_array = my_rank.astype(jnp.int32).reshape(1)
    pieces = []
    for head in range(0, head_width // HEAD_DIMENSION, PIECE_HEADS):
        piece = attend(rank_array, query, gathered, head, PIECE_HEADS)
        pieces.append([piece] + [from_group(piece, shift) for shift in range(1, head_groups)])
    w_out_cols = w_out_all.reshape(head_groups, fsdp_size // head_groups, *w_out.shape)
    group_array = current_group.astype(jnp.int32).reshape(1)
    before = []
    for index, piece in enumerate(pieces):
        out_type = jnp.bfloat16 if index == len(pieces) - 1 else jnp.float32
        before = [project(group_array, piece, w_out_cols, index, before, out_type)]
    (branch_cols,) = before
    own_cols = lax.dynamic_slice_in_dim(tokens, current_group * col_width, col_width, 1)
    resid = (own_cols.astype(jnp.float32) + branch_cols.astype(jnp.float32)).astype(jnp.bfloat16)

    top_count = routes.shape[1]
    experts_all = head_groups * fsdp_size
    capacity = max(2, 3 * tok_rows * top_count // (2 * experts_all))
    slots = experts_all * capacity
    expert_ids = jnp.arange(experts_all, dtype=jnp.int32)
    named = routes[:, :, None] == expert_ids[None, None, :]
    hits = jnp.any(named, axis=1)
    token_ids = jnp.arange(tok_rows, dtype=jnp.int32)
    earlier = (token_ids[None, :] < token_ids[:, None]).astype(jnp.bfloat16)
    rank = jnp.dot(earlier, hits.astype(jnp.bfloat16), preferred_element_type=jnp.float32)
    code = jnp.where(hits, rank, -1.0).astype(jnp.bfloat16)
    slot_list = jnp.arange(slots, dtype=jnp.int32)
    spread = (slot_list[None, :] // capacity == expert_ids[:, None]).astype(jnp.bfloat16)
    code_slots = jnp.dot(code, spread, preferred_element_type=jnp.float32)
    slot_match = code_slots == (slot_list % capacity).astype(jnp.float32)[None, :]
    chosen = slot_match.astype(jnp.bfloat16)
    named_probs = jnp.sum(jnp.where(named, route_probs[:, :, None], 0.0), axis=1)
    prob_slots = jnp.dot(
        named_probs.astype(jnp.bfloat16), spread, preferred_element_type=jnp.float32
    )
    mixing = lax.optimization_barrier(jnp.where(slot_match, prob_slots, 0.0).astype(jnp.bfloat16))

    outbound = lax.dot_general(
        chosen, resid, (((0,), (0,)), ((), ())), preferred_element_type=jnp.float32
    ).astype(jnp.bfloat16)
    arrived = lax.all_to_all(
        outbound.reshape(experts_all, capacity, col_width),
        ("grp", "fsdp"),
        split_axis=0,
        concat_axis=0,
        tiled=True,
    )
    arrived, branch_cols = lax.optimization_barrier((arrived, branch_cols))
    blocks = [branch_cols] + [from_group(branch_cols, shift) for shift in range(1, head_groups)]
    result = run_expert(
        arrived.reshape(head_groups, fsdp_size * capacity, col_width), ffn_gain, w_gate_up, w_down
    )
    result, blocks = lax.optimization_barrier((result, blocks))
    attn_branch = jnp.concatenate(
        [
            lax.select_n(lax.rem(group + head_groups - current_group, head_groups), *blocks)
            for group in range(head_groups)
        ],
        axis=1,
    )
    returned = lax.all_to_all(
        result.reshape(experts_all, capacity, col_width),
        ("grp", "fsdp"),
        split_axis=0,
        concat_axis=0,
        tiled=True,
    )
    expert_mix = jnp.dot(
        mixing, returned.reshape(slots, col_width), preferred_element_type=jnp.float32
    )
    layer_out = (resid.astype(jnp.float32) + expert_mix).astype(jnp.bfloat16)
    return (attn_branch, layer_out)


def solution(mesh):
    placed = (
        P("fsdp", None),
        P(),
        P(),
        P("fsdp", "grp"),
        P("fsdp", None),
        P("fsdp", None),
        P("grp", "fsdp"),
        P("fsdp", None),
        P("fsdp", None),
        P(("grp", "fsdp"), None, None),
        P(("grp", "fsdp"), None, None),
    )
    return jax.shard_map(
        on_device,
        mesh=mesh,
        in_specs=placed,
        out_specs=(P("fsdp", None), P("fsdp", "grp")),
        check_vma=False,
    )
```

```python
import functools

import jax
import jax.numpy as jnp
from jax import lax
from jax.experimental import pallas as pl
from jax.experimental.pallas import tpu as pltpu
from jax.sharding import PartitionSpec as P

KEY_VALUE_HEADS = 2
HEAD_DIMENSION = 128
FFW = 768


EPSILON = 1e-06
FLOOR_SCORE = -1e30
LOG2_E = 1.4426950408889634
SIDE = 4
PIECE_HEADS = 4
QUERY_TILE = 128
HIDDEN_TILE = 256
NORM_TILE = 64
EXPERT_VMEM = 40


def rms_scale(row_data, gain):
    floats = row_data.astype(jnp.float32)
    mean_sq = jnp.mean(floats * floats, axis=-1, keepdims=True)
    return (floats * lax.rsqrt(mean_sq + EPSILON) * gain).astype(jnp.bfloat16)


def to_other_core(rows):
    return lax.ppermute(rows, "fsdp", [(i, i ^ 1) for i in range(2 * SIDE * SIDE)])


def from_group(rows, shift):
    return lax.ppermute(rows, "grp", [((i + shift) % SIDE, i) for i in range(SIDE)])


def from_chips(rows):
    chips = SIDE * SIDE
    parts = lax.all_to_all(
        jnp.broadcast_to(rows[None], (chips, *rows.shape)),
        "fsdp",
        split_axis=0,
        concat_axis=0,
        axis_index_groups=[[2 * chip + core for chip in range(chips)] for core in range(2)],
        tiled=True,
    )
    return parts.reshape(chips * rows.shape[0], rows.shape[1])


def by_core(core, mine, other):
    return jnp.concatenate(
        [jnp.where(core == 0, mine, other), jnp.where(core == 0, other, mine)], axis=0
    )


def attend_kernel(
    rank_ref,
    query_ref,
    mine_ref,
    other_ref,
    out_ref,
    best,
    weighted,
    *,
    heads,
    first_head,
):
    rank = rank_ref[0]
    rows = query_ref.shape[0]
    span = 4 * rows
    core = rank % 2
    factor = HEAD_DIMENSION**-0.5 * LOG2_E
    best[...] = jnp.full_like(best, FLOOR_SCORE)
    weighted[...] = jnp.zeros_like(weighted)

    def step(index, masked):
        start = pl.multiple_of(index * span, span)
        mine = mine_ref[pl.ds(start, span), :]
        other = other_ref[pl.ds(start, span), :]
        keys = jnp.where(core == 0, mine, other)
        values = jnp.where(core == 0, other, mine)
        values = jnp.concatenate([values, jnp.ones_like(values)], axis=1)
        for head in range(heads):
            cols = slice((first_head + head) * HEAD_DIMENSION, (first_head + head + 1) * HEAD_DIMENSION)
            for row in range(0, rows, QUERY_TILE):
                tile = slice(row, row + QUERY_TILE)
                scores = lax.dot_general(
                    query_ref[tile, cols],
                    keys,
                    (((1,), (1,)), ((), ())),
                    preferred_element_type=jnp.float32,
                )
                if masked:
                    key_pos = lax.broadcasted_iota(jnp.int32, scores.shape, 1) + start
                    query_pos = lax.broadcasted_iota(jnp.int32, scores.shape, 0) + (
                        rank * rows + row
                    )
                    scores = jnp.where(key_pos <= query_pos, scores, FLOOR_SCORE)
                old = best[head, tile]
                new = jnp.maximum(old, jnp.max(scores, axis=1, keepdims=True))
                weights = jnp.exp2((scores - jnp.tile(new, (1, span // HEAD_DIMENSION))) * factor)
                rescale = jnp.exp2((old - new) * factor)
                best[head, tile] = new
                weighted[head, tile] = weighted[head, tile] * jnp.tile(rescale, (1, 2)) + jnp.dot(
                    weights.astype(jnp.bfloat16), values, preferred_element_type=jnp.float32
                )

    full = rank * rows // span

    def visit(index, carry):
        step(index, False)
        return carry

    lax.fori_loop(0, full, visit, 0)
    step(full, True)
    for head in range(heads):
        out_ref[:, head * HEAD_DIMENSION : (head + 1) * HEAD_DIMENSION] = (
            weighted[head, :, :HEAD_DIMENSION] / weighted[head, :, HEAD_DIMENSION:]
        ).astype(out_ref.dtype)


def attend(rank, query, gathered, first_head, heads):
    rows = query.shape[0]
    width = heads * HEAD_DIMENSION
    keys = gathered[0].shape[0]
    return pl.pallas_call(
        functools.partial(attend_kernel, heads=heads, first_head=first_head),
        out_shape=jax.ShapeDtypeStruct((rows, width), query.dtype),
        in_specs=[pl.BlockSpec(memory_space=pltpu.SMEM)]
        + [pl.BlockSpec(memory_space=pltpu.VMEM)] * (1 + len(gathered)),
        out_specs=pl.BlockSpec(memory_space=pltpu.VMEM),
        scratch_shapes=[
            pltpu.VMEM((heads, rows, HEAD_DIMENSION), jnp.float32),
            pltpu.VMEM((heads, rows, 2 * HEAD_DIMENSION), jnp.float32),
        ],
        compiler_params=pltpu.CompilerParams(vmem_limit_bytes=32 * 2**20),
        cost_estimate=pl.CostEstimate(
            flops=8 * rows * keys * width,
            bytes_accessed=4 * rows * width + 4 * keys * HEAD_DIMENSION,
            transcendentals=rows * keys * heads,
        ),
    )(rank, query, *gathered)


def project_kernel(group_ref, *refs, groups):
    part_refs, (weight_ref, *before, out_ref, total) = refs[:groups], refs[groups:]
    step = pl.program_id(0)
    blocks = weight_ref.shape[1]

    def times_weights(rows):
        return jnp.concatenate(
            [
                jnp.dot(
                    rows,
                    jnp.concatenate([weight_ref[0, i], weight_ref[0, i + 1]], axis=1),
                    preferred_element_type=jnp.float32,
                )
                for i in range(0, blocks, 2)
            ],
            axis=1,
        )

    for index in range(groups):

        @pl.when(step == index)
        def _(index=index):
            product = times_weights(part_refs[index][...])
            if index > 0:
                product += total[...]
            elif before:
                product += before[0][...]
            if index < groups - 1:
                total[...] = product
            else:
                out_ref[...] = product.astype(out_ref.dtype)


def project(group, parts, weights, piece, before, out_type):
    groups, blocks, _, block_cols = weights.shape
    rows, depth = parts[0].shape
    cols = blocks * block_cols
    whole = pl.BlockSpec((rows, cols), lambda i, group: (0, 0))
    return pl.pallas_call(
        functools.partial(project_kernel, groups=groups),
        grid_spec=pltpu.PrefetchScalarGridSpec(
            num_scalar_prefetch=1,
            grid=(groups,),
            in_specs=[pl.BlockSpec((rows, depth), lambda i, group: (0, 0))] * groups
            + [
                pl.BlockSpec(
                    (1, blocks, depth, block_cols),
                    lambda i, group: ((group[0] + i) % groups, 0, piece, 0),
                ),
            ]
            + [whole] * len(before),
            out_specs=whole,
            scratch_shapes=[pltpu.VMEM((rows, cols), jnp.float32)],
        ),
        out_shape=jax.ShapeDtypeStruct((rows, cols), out_type),
        compiler_params=pltpu.CompilerParams(vmem_limit_bytes=52 * 2**20),
        cost_estimate=pl.CostEstimate(
            flops=2 * groups * rows * depth * cols,
            bytes_accessed=2 * groups * depth * (rows + cols),
            transcendentals=0,
        ),
    )(group, *parts, weights, *before)


def expert_kernel(rows_ref, gain_ref, gate_ref, up_ref, down_ref, out_ref, normed, hidden, *, wide):
    step = pl.program_id(0)
    parts, rows, width = rows_ref.shape

    @pl.when(step == 0)
    def _():
        def scale_rows(index, carry):
            tile = pl.ds(pl.multiple_of(index * NORM_TILE, NORM_TILE), NORM_TILE)
            floats = [rows_ref[part, tile, :].astype(jnp.float32) for part in range(parts)]
            squares = sum(values * values for values in floats)
            mean_sq = jnp.sum(squares, axis=1, keepdims=True) / (parts * width)
            scale = lax.rsqrt(mean_sq + EPSILON)
            for part in range(parts):
                normed[part, tile, :] = (floats[part] * scale * gain_ref[part]).astype(jnp.bfloat16)
            return carry

        lax.fori_loop(0, rows // NORM_TILE, scale_rows, 0)

    @pl.when(step < wide)
    def _():
        def project(weight_ref):
            return sum(
                jnp.dot(
                    normed[part],
                    weight_ref[0, part * width : (part + 1) * width, :],
                    preferred_element_type=jnp.float32,
                )
                for part in range(parts)
            )

        hidden[step] = (jax.nn.silu(project(gate_ref)) * project(up_ref)).astype(jnp.bfloat16)

    @pl.when(step >= wide)
    def _():
        out_ref[0] = sum(
            jnp.dot(
                hidden[tile],
                down_ref[0, tile * HIDDEN_TILE : (tile + 1) * HIDDEN_TILE, :],
                preferred_element_type=jnp.float32,
            )
            for tile in range(wide)
        ).astype(out_ref.dtype)


def run_expert(arrived, gain, w_gate_up, w_down):
    parts, rows, width = arrived.shape
    model_width = parts * width
    wide = FFW // HIDDEN_TILE
    return pl.pallas_call(
        functools.partial(expert_kernel, wide=wide),
        grid=(wide + parts,),
        out_shape=pltpu.HBM(arrived.shape, arrived.dtype),
        in_specs=[
            pl.BlockSpec(memory_space=pltpu.VMEM),
            pl.BlockSpec(memory_space=pltpu.VMEM),
            pl.BlockSpec((1, model_width, HIDDEN_TILE), lambda i: (0, 0, jnp.minimum(i, wide - 1))),
            pl.BlockSpec(
                (1, model_width, HIDDEN_TILE), lambda i: (0, 0, wide + jnp.minimum(i, wide - 1))
            ),
            pl.BlockSpec((1, FFW, width), lambda i: (0, 0, jnp.maximum(i - wide, 0))),
        ],
        out_specs=pl.BlockSpec((1, rows, width), lambda i: (jnp.maximum(i - wide, 0), 0, 0)),
        scratch_shapes=[
            pltpu.VMEM((parts, rows, width), jnp.bfloat16),
            pltpu.VMEM((wide, rows, HIDDEN_TILE), jnp.bfloat16),
        ],
        compiler_params=pltpu.CompilerParams(vmem_limit_bytes=EXPERT_VMEM * 2**20),
        cost_estimate=pl.CostEstimate(
            flops=6 * rows * model_width * FFW,
            bytes_accessed=4 * rows * model_width + 6 * model_width * FFW,
            transcendentals=rows * FFW,
        ),
    )(arrived, gain.reshape(parts, 1, width), w_gate_up, w_gate_up, w_down)


def on_device(
    tokens,
    attn_gain,
    ffn_gain,
    w_query,
    w_key,
    value_weight,
    w_out,
    routes,
    route_probs,
    w_gate_up,
    w_down,
):
    head_groups = lax.axis_size("grp")
    fsdp_size = lax.axis_size("fsdp")
    current_group = lax.axis_index("grp")
    my_rank = lax.axis_index("fsdp")
    tok_rows, model_width = tokens.shape
    head_width = w_query.shape[1]
    col_width = model_width // head_groups
    key_value_head = current_group * KEY_VALUE_HEADS // head_groups
    key_cols = lax.dynamic_slice_in_dim(w_key, key_value_head * HEAD_DIMENSION, HEAD_DIMENSION, 1)
    value_cols = lax.dynamic_slice_in_dim(
        value_weight, key_value_head * HEAD_DIMENSION, HEAD_DIMENSION, 1
    )
    core = my_rank % 2
    w_query_all = lax.all_gather(w_query, "fsdp", axis=0, tiled=True)
    normed = lax.optimization_barrier(rms_scale(tokens, attn_gain))
    normed_other = to_other_core(normed)
    w_both, normed = lax.optimization_barrier((jnp.stack([key_cols, value_cols]), normed))
    w_kv = lax.all_to_all(
        jnp.tile(w_both, (fsdp_size // 2, 1, 1)), "fsdp", split_axis=0, concat_axis=0, tiled=True
    ).reshape(model_width, HEAD_DIMENSION)

    def project_kv(rows):
        return jnp.dot(rows, w_kv, preferred_element_type=jnp.float32).astype(jnp.bfloat16)

    kv_local = by_core(core, project_kv(normed), project_kv(normed_other))
    w_out_block, w_kv = lax.optimization_barrier((w_out, w_kv))
    w_turned = lax.ppermute(
        w_out_block,
        ("grp", "fsdp"),
        [
            (g * fsdp_size + f, f // 8 * fsdp_size + g * 8 + f % 8)
            for g in range(head_groups)
            for f in range(fsdp_size)
        ],
    )
    w_turned, kv_local = lax.optimization_barrier((w_turned, kv_local))
    w_out_all = lax.all_gather(w_turned, "fsdp", axis=0, tiled=True)
    kv_mine = from_chips(kv_local)
    piece_cols = PIECE_HEADS * HEAD_DIMENSION
    queries = [
        jnp.dot(
            normed, w_query_all[:, start : start + piece_cols], preferred_element_type=jnp.float32
        ).astype(jnp.bfloat16)
        for start in range(0, head_width, piece_cols)
    ]
    kv_mine, queries = lax.optimization_barrier((kv_mine, queries))
    gathered = (kv_mine, to_other_core(kv_mine))
    rank_array = my_rank.astype(jnp.int32).reshape(1)
    pieces = []
    for query in queries:
        piece = attend(rank_array, query, gathered, 0, PIECE_HEADS)
        pieces.append([piece] + [from_group(piece, shift) for shift in range(1, head_groups)])
    w_out_cols = w_out_all.reshape(head_groups, fsdp_size // head_groups, *w_out.shape)
    group_array = current_group.astype(jnp.int32).reshape(1)
    before = []
    for index, piece in enumerate(pieces):
        out_type = jnp.bfloat16 if index == len(pieces) - 1 else jnp.float32
        before = [project(group_array, piece, w_out_cols, index, before, out_type)]
    (branch_cols,) = before
    own_cols = lax.dynamic_slice_in_dim(tokens, current_group * col_width, col_width, 1)
    resid = (own_cols.astype(jnp.float32) + branch_cols.astype(jnp.float32)).astype(jnp.bfloat16)

    top_count = routes.shape[1]
    experts_all = head_groups * fsdp_size
    capacity = max(2, 3 * tok_rows * top_count // (2 * experts_all))
    slots = experts_all * capacity
    expert_ids = jnp.arange(experts_all, dtype=jnp.int32)
    named = routes[:, :, None] == expert_ids[None, None, :]
    hits = jnp.any(named, axis=1)
    token_ids = jnp.arange(tok_rows, dtype=jnp.int32)
    earlier = (token_ids[None, :] < token_ids[:, None]).astype(jnp.bfloat16)
    rank = jnp.dot(earlier, hits.astype(jnp.bfloat16), preferred_element_type=jnp.float32)
    code = jnp.where(hits, rank, -1.0).astype(jnp.bfloat16)
    slot_list = jnp.arange(slots, dtype=jnp.int32)
    spread = (slot_list[None, :] // capacity == expert_ids[:, None]).astype(jnp.bfloat16)
    code_slots = jnp.dot(code, spread, preferred_element_type=jnp.float32)
    slot_match = code_slots == (slot_list % capacity).astype(jnp.float32)[None, :]
    chosen = slot_match.astype(jnp.bfloat16)
    named_probs = jnp.sum(jnp.where(named, route_probs[:, :, None], 0.0), axis=1)
    prob_slots = jnp.dot(
        named_probs.astype(jnp.bfloat16), spread, preferred_element_type=jnp.float32
    )
    mixing = lax.optimization_barrier(jnp.where(slot_match, prob_slots, 0.0).astype(jnp.bfloat16))

    outbound = lax.dot_general(
        chosen, resid, (((0,), (0,)), ((), ())), preferred_element_type=jnp.float32
    ).astype(jnp.bfloat16)
    arrived = lax.all_to_all(
        outbound.reshape(experts_all, capacity, col_width),
        ("grp", "fsdp"),
        split_axis=0,
        concat_axis=0,
        tiled=True,
    )
    arrived, branch_cols = lax.optimization_barrier((arrived, branch_cols))
    blocks = [branch_cols] + [from_group(branch_cols, shift) for shift in range(1, head_groups)]
    result = run_expert(
        arrived.reshape(head_groups, fsdp_size * capacity, col_width), ffn_gain, w_gate_up, w_down
    )
    result, blocks = lax.optimization_barrier((result, blocks))
    attn_branch = jnp.concatenate(
        [
            lax.select_n(lax.rem(group + head_groups - current_group, head_groups), *blocks)
            for group in range(head_groups)
        ],
        axis=1,
    )
    returned = lax.all_to_all(
        result.reshape(experts_all, capacity, col_width),
        ("grp", "fsdp"),
        split_axis=0,
        concat_axis=0,
        tiled=True,
    )
    expert_mix = jnp.dot(
        mixing, returned.reshape(slots, col_width), preferred_element_type=jnp.float32
    )
    layer_out = (resid.astype(jnp.float32) + expert_mix).astype(jnp.bfloat16)
    return (attn_branch, layer_out)


def solution(mesh):
    placed = (
        P("fsdp", None),
        P(),
        P(),
        P("fsdp", "grp"),
        P("fsdp", None),
        P("fsdp", None),
        P("grp", "fsdp"),
        P("fsdp", None),
        P("fsdp", None),
        P(("grp", "fsdp"), None, None),
        P(("grp", "fsdp"), None, None),
    )
    return jax.shard_map(
        on_device,
        mesh=mesh,
        in_specs=placed,
        out_specs=(P("fsdp", None), P("fsdp", "grp")),
        check_vma=False,
    )
```
